512 devices in a mesh: cuts: 2 (over core), dp: 128 (over x, y_lo, z), mp: 2 (over y_hi).
Axes of the slice: x: 4, y: 8 (y_hi: 2, y_lo: 4; y = y_hi * 4 + y_lo), z: 8, core: 2. Of those that a mesh axis runs over, the one named last changes fastest.
Arguments:
- hidden: bfloat16 [512, 128, 14336], P(('cuts', 'dp'), None, 'mp'), may hold values from -6 to 6
- out_grads: bfloat16 [512, 128, 4096], P(('cuts', 'dp'), None, 'mp'), may hold values from -70 to 70
- lengths: int32 [512], P(('cuts', 'dp')), may hold values from 1 to 128, 49152 in all
- queries: bfloat16 [256, 4096], P('dp'), may hold values from -6 to 6
- proj_seeds: int32 [2], replicated, may hold values from 0 to 1048575
Outputs:
- influence: float32 [512, 256], P(('cuts', 'dp'))
The draws below stay inside these ranges and needn't reach their ends.
Inputs may be any that keep to these rules, and one draw needn't show every extreme that they name: Positions 0 to lengths[e] - 1 of training example e are its tokens; the rest are padding.
All inputs are finite; a program needn't handle non-finite values. No bound on the sum of `lengths` on one device may be relied on, other than what follows from the above.
Results may differ from the reference program's by a relative error of at most 0.0003.
Values may be sent and summed in bfloat16 or wider, within the bound.
No kernel may reach another device: no remote copies, remote signals or barrier semaphores. Data moves between devices by JAX's collectives and lax.ppermute only.
A program may use at most 64 MiB of HBM per device.

```python
import math
import jax
import jax.numpy as jnp
import numpy as np
from jax import lax

D = 4096
FF = 14336
CODE = 64
SEQ = 128
TRAIN_EX = 512
QUERIES = 256


def draw_out_grads(key, part):
    key = jax.random.fold_in(key, 7)
    key_base = jax.random.fold_in(key, 1)
    key_spread = jax.random.fold_in(key, 2)
    example_ids = lax.broadcasted_iota(jnp.float32, (TRAIN_EX, SEQ, 1), 0)
    rising = jnp.exp(math.log(3.0) * example_ids / max(TRAIN_EX - 1, 1))
    spread_draw = jax.random.uniform(key_spread, (TRAIN_EX, SEQ, 1), jnp.float32)
    base_values = 0.3 * jnp.clip(jax.random.normal(key_base, (TRAIN_EX, SEQ, D), jnp.float32), -6.0, 6.0)
    token_scale = jnp.exp(math.log(10.0) * spread_draw)
    return (base_values * token_scale * rising).astype(jnp.bfloat16)


def levels(own_key, shape, pieces, least, top_value):
    gain = 1.0
    for dim, blocks in pieces:
        heights = jax.random.uniform(jax.random.fold_in(jax.random.fold_in(own_key, 6), dim), (blocks,), jnp.float32, least / len(pieces), top_value / len(pieces))
        gain = gain * jnp.repeat(jnp.exp(heights), shape[dim] // blocks).reshape((-1,) + (1,) * (len(shape) - 1 - dim))
    return gain


def length_profile(count, total, limit, skew):
    loads = [(1 << 20) // math.isqrt(grade ** skew) + 1 for grade in range(2, count + 1)]
    rest, holding = total - limit - (count - 1), [1] * (count - 1)
    while rest > 0:
        free = [i for i in range(count - 1) if holding[i] < limit]
        mass, left = sum([loads[i] for i in free]), rest
        for i in free:
            more = min(limit - holding[i], max(1, left * loads[i] // mass), rest)
            holding[i] = holding[i] + more
            rest = rest - more
    return np.array([limit] + holding)


def uneven_parts(rng, number_of, total, reach, lean):
    if number_of == 2:
        one = jax.random.randint(rng, (), max(1, total - reach), min(reach, total - 1) + 1)
        return jnp.stack([one, total - one])
    sizes = jnp.asarray(length_profile(number_of, total, reach, lean), jnp.int32)
    pairs = (number_of - 1) // 2
    source_of, sink = sizes[1:1 + 2 * pairs:2], sizes[2:2 + 2 * pairs:2]
    slack = jnp.minimum(source_of - 1, reach - sink)
    moved = jax.random.randint(jax.random.fold_in(rng, 1), (pairs,), 0, 1 << 20) % (slack + 1)
    sizes = sizes.at[1:1 + 2 * pairs:2].set(source_of - moved).at[2:2 + 2 * pairs:2].set(sink + moved)
    return sizes[jax.random.permutation(jax.random.fold_in(rng, 2), number_of)]


def noise(stream_key, dims, scale, limit, split=(), kind=jnp.bfloat16):
    factor_of = levels(stream_key, dims, split, -0.22, 0.18) if split else 1.0
    values = jax.random.normal(stream_key, dims, jnp.float32) * scale * factor_of
    return jnp.minimum(jnp.maximum(values, -limit), limit).astype(kind)


def setup_inputs(seed: int = 0) -> dict:
    key_list = jax.random.split(jax.random.key(seed), 6)
    hidden = noise(key_list[0], (TRAIN_EX, SEQ, FF), 1.0, 6.0, ((0, 256), (2, 2)))
    out_grads = draw_out_grads(jax.random.fold_in(key_list[5], 71), 0)
    lengths = uneven_parts(key_list[2], TRAIN_EX, TRAIN_EX * (SEQ * 3 // 4), SEQ, 1).astype(jnp.int32)
    queries = noise(key_list[3], (QUERIES, CODE * CODE), 1.0, 6.0, ((0, 128),))
    proj_seeds = jax.random.randint(key_list[4], (2,), 0, 1048576).astype(jnp.int32)
    return {"hidden": hidden, "out_grads": out_grads, "lengths": lengths, "queries": queries, "proj_seeds": proj_seeds}


damping = 0.1

def sign_table(seed_value, row_start, row_count, code_width):
    row_ids = lax.broadcasted_iota(jnp.int32, (row_count, code_width), 0) + row_start
    col_ids = lax.broadcasted_iota(jnp.int32, (row_count, code_width), 1)
    hashed = row_ids * 73856093 ^ col_ids * 19349663 ^ seed_value * 83492791
    hashed = hashed ^ lax.shift_right_logical(hashed, jnp.int32(13))
    hashed = hashed * 1274126177
    hashed = hashed ^ lax.shift_right_logical(hashed, jnp.int32(16))
    sign_bit = lax.shift_right_logical(hashed, jnp.int32(7)) & 1
    return (1 - 2 * sign_bit).astype(jnp.float32).astype(jnp.bfloat16)

def make_codes(in_proj, out_proj, lengths, offset):
    positions = lax.broadcasted_iota(jnp.int32, (in_proj.shape[0], in_proj.shape[1]), 1) + offset
    valid_mask = (positions < lengths[:, None]).astype(jnp.float32)
    weights = valid_mask / lengths[:, None].astype(jnp.float32)
    return jnp.einsum('eto,eti->eoi', out_proj * weights[:, :, None], in_proj, precision=lax.Precision.HIGHEST)

def inverses(out_factor, in_factor):
    total_trace = jnp.trace(out_factor)
    identity = jnp.eye(CODE, dtype=jnp.float32)
    out_damped = out_factor * (CODE / total_trace) + damping * identity
    in_damped = in_factor * (CODE / total_trace) + damping * identity
    out_lower = jnp.linalg.cholesky(out_damped)
    in_lower = jnp.linalg.cholesky(in_damped)
    out_inverse = jax.scipy.linalg.cho_solve((out_lower, True), identity)
    in_inverse = jax.scipy.linalg.cho_solve((in_lower, True), identity)
    return (out_inverse, in_inverse)

def reference(hidden, out_grads, lengths, queries, proj_seeds):
    in_table = sign_table(proj_seeds[0], 0, FF, CODE)
    out_table = sign_table(proj_seeds[1], 0, D, CODE)
    in_proj = jnp.dot(hidden.reshape(-1, FF).astype(jnp.float32), in_table.astype(jnp.float32), preferred_element_type=jnp.float32) * (1.0 / math.sqrt(FF))
    out_proj = jnp.dot(out_grads.reshape(-1, D).astype(jnp.float32), out_table.astype(jnp.float32), preferred_element_type=jnp.float32) * (1.0 / math.sqrt(D))
    in_proj = in_proj.reshape(TRAIN_EX, SEQ, CODE)
    out_proj = out_proj.reshape(TRAIN_EX, SEQ, CODE)
    train_codes = make_codes(in_proj, out_proj, lengths, 0)
    out_factor = jnp.einsum('eab,ecb->ac', train_codes, train_codes, precision=lax.Precision.HIGHEST)
    in_factor = jnp.einsum('eba,ebc->ac', train_codes, train_codes, precision=lax.Precision.HIGHEST)
    out_inverse, in_inverse = inverses(out_factor, in_factor)
    query_codes = queries.astype(jnp.float32).reshape(QUERIES, CODE, CODE)
    conditioned = jnp.einsum('ab,nbc,cd->nad', out_inverse, query_codes, in_inverse, precision=lax.Precision.HIGHEST)
    train_flat = train_codes.reshape(TRAIN_EX, CODE * CODE)
    cond_flat = conditioned.reshape(QUERIES, CODE * CODE)
    return jnp.dot(train_flat, cond_flat.T, precision=lax.Precision.HIGHEST) * (1.0 / math.sqrt(CODE))
```

```python
import math

import jax
import jax.numpy as jnp
from jax import lax
from jax.experimental import pallas as pl
from jax.experimental.pallas import tpu as pltpu
from jax.sharding import Mesh, PartitionSpec as P

D = 4096
FF = 14336
CODE = 64
DAMPING = 0.1
STEPS = 4
HIGH = lax.Precision.HIGHEST
F32 = jnp.float32
I32 = jnp.int32


def dot(a, b, dims, precision=HIGH):
    return lax.dot_general(
        a, b, (dims, ((), ())), precision=precision, preferred_element_type=F32
    )


def sign_rows(seed, first, count):
    rows = lax.broadcasted_iota(I32, (1, count), 1) + first
    cols = lax.broadcasted_iota(I32, (CODE, 1), 0)
    hashed = (rows * 73856093 ^ seed * 83492791) ^ (cols * 19349663)
    hashed = hashed ^ lax.shift_right_logical(hashed, jnp.int32(13))
    hashed = hashed * 1274126177
    hashed = hashed ^ lax.shift_right_logical(hashed, jnp.int32(16))
    return jnp.where((hashed & 128) == 0, 1.0, -1.0).astype(jnp.bfloat16)


def project_kernel(place_ref, hidden_ref, grads_ref, part_ref):
    step = pl.program_id(0)
    half = place_ref[2]
    ff_block = hidden_ref.shape[1]
    d_block = grads_ref.shape[1]
    in_rows = sign_rows(place_ref[0], (half * STEPS + step) * ff_block, ff_block)
    out_rows = sign_rows(place_ref[1], (half * STEPS + step) * d_block, d_block)
    in_rows = jnp.concatenate([jnp.zeros_like(in_rows), in_rows], axis=0)
    out_rows = jnp.concatenate([out_rows, jnp.zeros_like(out_rows)], axis=0)
    nt = ((1,), (1,))
    part = dot(hidden_ref[...], in_rows, nt, None) + dot(grads_ref[...], out_rows, nt, None)

    @pl.when(step == 0)
    def _():
        part_ref[...] = part

    @pl.when(step > 0)
    def _():
        part_ref[...] += part


def project(place, hidden, grads):
    rows, ff_local = hidden.shape
    d_local = grads.shape[1]
    return pl.pallas_call(
        project_kernel,
        grid=(STEPS,),
        in_specs=[
            pl.BlockSpec(memory_space=pltpu.SMEM),
            pl.BlockSpec((rows, ff_local // STEPS), lambda s: (0, s)),
            pl.BlockSpec((rows, d_local // STEPS), lambda s: (0, s)),
        ],
        out_specs=pl.BlockSpec((rows, 2 * CODE), lambda s: (0, 0)),
        out_shape=jax.ShapeDtypeStruct((rows, 2 * CODE), F32),
        compiler_params=pltpu.CompilerParams(vmem_limit_bytes=32 * 2**20),
        name="project",
    )(place, hidden, grads)


def codes_kernel(lengths_ref, own_ref, other_ref, codes_ref, packed_ref):
    total = own_ref[...] + other_ref[...]
    tokens = total.shape[0] // 2
    position = lax.broadcasted_iota(I32, (tokens, 1), 0)
    codes = []
    for e in range(2):
        length = lengths_ref[e]
        scale = (1.0 / math.sqrt(D)) * (1.0 / math.sqrt(FF))
        weight = jnp.where(position < length, scale / length.astype(F32), 0.0)
        part = total[e * tokens : (e + 1) * tokens]
        both = dot(part * weight, part, ((0,), (0,)))
        codes.append(both[:CODE, CODE:])
    wide = jnp.concatenate(codes, axis=1)
    tall = jnp.concatenate(codes, axis=0)
    codes_ref[...] = wide
    out_factor = dot(wide, wide, ((1,), (1,)))
    in_factor = dot(tall, tall, ((0,), (0,)))
    row = lax.broadcasted_iota(I32, (CODE, CODE), 0)
    col = lax.broadcasted_iota(I32, (CODE, CODE), 1)
    square = jnp.where(col >= row, out_factor, in_factor)
    half = CODE // 2
    packed_ref[:half] = jnp.concatenate([square[:half], square[half:]], axis=1)
    diagonal = jnp.sum(jnp.where(row == col, in_factor, 0.0), axis=0, keepdims=True)
    tail = jnp.concatenate([diagonal, jnp.zeros_like(diagonal)], axis=1)
    packed_ref[half:] = jnp.broadcast_to(tail, (8, 2 * CODE))


VMEM = pl.BlockSpec(memory_space=pltpu.VMEM)
SMEM = pl.BlockSpec(memory_space=pltpu.SMEM)
PACKED = (CODE // 2 + 8, 2 * CODE)


def make_codes(lengths, own, other):
    return pl.pallas_call(
        codes_kernel,
        in_specs=[SMEM, VMEM, VMEM],
        out_specs=[VMEM, VMEM],
        out_shape=[
            jax.ShapeDtypeStruct((CODE, 2 * CODE), F32),
            jax.ShapeDtypeStruct(PACKED, F32),
        ],
        name="codes",
    )(lengths, own, other)


def add_kernel(*refs):
    copies_ref = refs[-1]
    if len(refs) == 3:
        total = refs[0][...] + refs[1][...]
    else:
        total = refs[0][0]
        for i in range(1, refs[0].shape[0]):
            total = total + refs[0][i]
    for i in range(copies_ref.shape[0]):
        copies_ref[i] = total


def add_and_copy(count, *arrays):
    return pl.pallas_call(
        add_kernel,
        in_specs=[VMEM] * len(arrays),
        out_specs=VMEM,
        out_shape=jax.ShapeDtypeStruct((count,) + PACKED, F32),
        name="add",
    )(*arrays)


def solve_kernel(parts_ref, codes_ref, queries_ref, out_ref, held, sums, rows_ref, sem):
    copy = pltpu.make_async_copy(queries_ref, held, sem)
    copy.start()
    packed = parts_ref[0]
    for i in range(1, parts_ref.shape[0]):
        packed = packed + parts_ref[i]
    half = CODE // 2
    square = jnp.concatenate([packed[:half, :CODE], packed[:half, CODE:]], axis=0)
    row = lax.broadcasted_iota(I32, (CODE, CODE), 0)
    col = lax.broadcasted_iota(I32, (CODE, CODE), 1)
    upper = jnp.where(col > row, square, 0.0)
    lower = jnp.where(col < row, square, 0.0)
    diagonal = jnp.where(col == row, square, 0.0)
    trace = jnp.sum(diagonal)
    out_factor = upper + upper.T + diagonal
    in_factor = lower + lower.T + jnp.where(col == row, packed[half : half + 1, :CODE], 0.0)

    row = lax.broadcasted_iota(I32, (CODE, 2 * CODE), 0)
    lane = lax.broadcasted_iota(I32, (CODE, 2 * CODE), 1)
    place = jnp.where(lane < CODE, lane, lane - CODE)
    grid = jnp.concatenate([out_factor, in_factor], axis=1) * (CODE / trace)
    grid = grid + jnp.where(place == row, DAMPING, 0.0)
    for k in range(CODE):
        column = jnp.where(
            lane < CODE, grid[:, k : k + 1], grid[:, CODE + k : CODE + k + 1]
        )
        inverse = 1.0 / column[k : k + 1]
        pivot_row = jnp.where(place[:1] == k, inverse, grid[k : k + 1] * inverse)
        grid = jnp.where(place == k, 0.0, grid) - column * pivot_row
        grid = jnp.where(row == k, pivot_row, grid)

    out_inverse = grid[:, :CODE]
    in_inverse = grid[:, CODE:]
    nn = ((1,), (0,))
    left = dot(out_inverse, codes_ref[...], nn)
    score_scale = 1.0 / math.sqrt(CODE)
    scaled = in_inverse * score_scale
    rows_ref[:, :CODE] = dot(left[:, :CODE], scaled, nn)
    rows_ref[:, CODE:] = dot(left[:, CODE:], scaled, nn)
    even = rows_ref[pl.ds(0, half, stride=2), :]
    odd = rows_ref[pl.ds(1, half, stride=2), :]
    flat = [
        jnp.concatenate([even[:, :CODE], odd[:, :CODE]], axis=1),
        jnp.concatenate([even[:, CODE:], odd[:, CODE:]], axis=1),
    ]
    copy.wait()
    block = 32
    width = 2 * CODE
    for b in range(held.shape[0] // block):
        total = [jnp.zeros((block, width), F32), jnp.zeros((block, width), F32)]
        for j in range(half):
            piece = held[b * block : (b + 1) * block, j * width : (j + 1) * width].astype(F32)
            for e in range(2):
                total[e] = total[e] + piece * flat[e][j : j + 1]
        for e in range(2):
            sums[e, b * block : (b + 1) * block] = total[e]
    count = held.shape[0]
    came = lax.broadcasted_iota(I32, (count, count), 0)
    goes = lax.broadcasted_iota(I32, (count, count), 1)
    z, xy, own = came // 32, (came // 2) % 16, came % 2
    swap = jnp.where((xy * 8 + z) * 2 + own == goes, 1.0, 0.0)
    ones = jnp.ones((8, width), F32)
    for e in range(2):
        line = dot(ones, sums[e], ((1,), (1,)))
        out_ref[e : e + 1] = dot(line, swap, nn)[:1]


def solve(parts, codes, queries):
    count = queries.shape[0]
    return pl.pallas_call(
        solve_kernel,
        in_specs=[VMEM, VMEM, pl.BlockSpec(memory_space=pl.ANY)],
        out_specs=VMEM,
        out_shape=jax.ShapeDtypeStruct((2, count), F32),
        scratch_shapes=[
            pltpu.VMEM(queries.shape, queries.dtype),
            pltpu.VMEM((2, count, 2 * CODE), F32),
            pltpu.VMEM((CODE, 2 * CODE), F32),
            pltpu.SemaphoreType.DMA,
        ],
        compiler_params=pltpu.CompilerParams(vmem_limit_bytes=32 * 2**20),
        name="solve",
    )(parts, codes, queries)


SWAP = [(0, 1), (1, 0)]


def on_device(hidden, out_grads, lengths, queries, proj_seeds):
    examples, seq_len, ff_local = hidden.shape
    d_local = out_grads.shape[2]
    copies = jnp.broadcast_to(queries[None], (16,) + queries.shape)
    near = lax.all_to_all(copies, ("x", "y"), 0, 0)
    near = near.reshape(-1, CODE * CODE)
    all_queries = lax.all_gather(near, "z", axis=0, tiled=True)

    place = jnp.concatenate([proj_seeds, lax.axis_index("mp")[None].astype(I32)])
    own = project(
        place, hidden.reshape(-1, ff_local), out_grads.reshape(-1, d_local)
    )
    other = lax.ppermute(own, "mp", SWAP)
    codes, packed = make_codes(lengths, own, other)
    copies = add_and_copy(16, packed, lax.ppermute(packed, "cuts", SWAP))
    copies = add_and_copy(8, lax.all_to_all(copies, ("x", "y"), 0, 0))
    parts = lax.all_to_all(copies, "z", 0, 0)
    return solve(parts, codes, all_queries)


def solution(mesh):
    fine = Mesh(mesh.devices.reshape(2, 4, 4, 8, 2), ("cuts", "x", "y", "z", "mp"))
    rows = ("cuts", "x", "y", "z")
    return jax.shard_map(
        on_device,
        mesh=fine,
        in_specs=(
            P(rows, None, "mp"),
            P(rows, None, "mp"),
            P(rows),
            P(("x", "y", "z"), None),
            P(),
        ),
        out_specs=P(rows, None),
        check_vma=False,
    )
```

```python
import math

import jax
import jax.numpy as jnp
from jax import lax
from jax.experimental import pallas as pl
from jax.experimental.pallas import tpu as pltpu
from jax.sharding import Mesh, PartitionSpec as P

D = 4096
FF = 14336
CODE = 64
DAMPING = 0.1
STEPS = 4
HIGH = lax.Precision.HIGHEST
F32 = jnp.float32
I32 = jnp.int32
VMEM = pl.BlockSpec(memory_space=pltpu.VMEM)
SMEM = pl.BlockSpec(memory_space=pltpu.SMEM)
PACKED = (CODE // 2 + 8, 2 * CODE)
SMALL = pltpu.CompilerParams(vmem_limit_bytes=4 * 2**20)


def dot(a, b, dims, precision=HIGH):
    return lax.dot_general(
        a, b, (dims, ((), ())), precision=precision, preferred_element_type=F32
    )


def sign_rows(seed, first, count):
    rows = lax.broadcasted_iota(I32, (1, count), 1) + first
    cols = lax.broadcasted_iota(I32, (CODE, 1), 0)
    hashed = (rows * 73856093 ^ seed * 83492791) ^ (cols * 19349663)
    hashed = hashed ^ lax.shift_right_logical(hashed, jnp.int32(13))
    hashed = hashed * 1274126177
    hashed = hashed ^ lax.shift_right_logical(hashed, jnp.int32(16))
    return jnp.where((hashed & 128) == 0, 1.0, -1.0).astype(jnp.bfloat16)


def project_kernel(seeds_ref, hidden_ref, grads_ref, part_ref, hidden_vmem, grads_vmem, sems):
    half = lax.axis_index("mp")
    rows, ff_local = hidden_ref.shape
    d_local = grads_ref.shape[1]
    ff_block = ff_local // STEPS
    pieces = [(grads_ref, grads_vmem, 0, d_local)]
    for i in range(STEPS):
        pieces.append((hidden_ref, hidden_vmem, i * ff_block, ff_block))
    copies = []
    for i, (source, held, first, count) in enumerate(pieces):
        columns = pl.ds(first, count)
        copies.append(
            pltpu.make_async_copy(source.at[:, columns], held.at[:, columns], sems.at[i])
        )
        copies[-1].start()
    total = jnp.zeros((rows, 2 * CODE), F32)
    for i, (source, held, first, count) in enumerate(pieces):
        of_grads = i == 0
        seed = seeds_ref[1] if of_grads else seeds_ref[0]
        whole = d_local if of_grads else ff_local
        table = sign_rows(seed, half * whole + first, count)
        empty = jnp.zeros_like(table)
        table = jnp.concatenate([table, empty] if of_grads else [empty, table], axis=0)
        copies[i].wait()
        total = total + dot(held[:, first : first + count], table, ((1,), (1,)), None)
    part_ref[...] = total


def project(seeds, hidden, grads):
    hbm = pl.BlockSpec(memory_space=pltpu.HBM)
    return pl.pallas_call(
        project_kernel,
        in_specs=[SMEM, hbm, hbm],
        out_specs=VMEM,
        out_shape=jax.ShapeDtypeStruct((hidden.shape[0], 2 * CODE), F32),
        scratch_shapes=[
            pltpu.VMEM(hidden.shape, hidden.dtype),
            pltpu.VMEM(grads.shape, grads.dtype),
            pltpu.SemaphoreType.DMA((STEPS + 1,)),
        ],
        compiler_params=pltpu.CompilerParams(vmem_limit_bytes=63 * 2**20),
        name="project",
    )(seeds, hidden, grads)


def codes_kernel(lengths_ref, own_ref, other_ref, made_ref):
    total = own_ref[...] + other_ref[...]
    tokens = total.shape[0] // 2
    position = lax.broadcasted_iota(I32, (tokens, 1), 0)
    codes = []
    for e in range(2):
        length = lengths_ref[e]
        scale = (1.0 / math.sqrt(D)) * (1.0 / math.sqrt(FF))
        weight = jnp.where(position < length, scale / length.astype(F32), 0.0)
        part = total[e * tokens : (e + 1) * tokens]
        both = dot(part * weight, part, ((0,), (0,)))
        codes.append(both[:CODE, CODE:])
    wide = jnp.concatenate(codes, axis=1)
    tall = jnp.concatenate(codes, axis=0)
    made_ref[PACKED[0] :] = wide
    out_factor = dot(wide, wide, ((1,), (1,)))
    in_factor = dot(tall, tall, ((0,), (0,)))
    row = lax.broadcasted_iota(I32, (CODE, CODE), 0)
    col = lax.broadcasted_iota(I32, (CODE, CODE), 1)
    square = jnp.where(col >= row, out_factor, in_factor)
    half = CODE // 2
    made_ref[:half] = jnp.concatenate([square[:half], square[half:]], axis=1)
    diagonal = jnp.sum(jnp.where(row == col, in_factor, 0.0), axis=0, keepdims=True)
    tail = jnp.concatenate([diagonal, jnp.zeros_like(diagonal)], axis=1)
    made_ref[half : PACKED[0]] = jnp.broadcast_to(tail, (8, 2 * CODE))


def repeat_kernel(array_ref, copies_ref):
    for i in range(copies_ref.shape[0]):
        copies_ref[i] = array_ref[...]


def repeat(array, count):
    return pl.pallas_call(
        repeat_kernel,
        in_specs=[VMEM],
        out_specs=VMEM,
        out_shape=jax.ShapeDtypeStruct((count,) + array.shape, array.dtype),
        compiler_params=SMALL,
        name="repeat",
    )(array)


def make_codes(lengths, own, other):
    return pl.pallas_call(
        codes_kernel,
        in_specs=[SMEM, VMEM, VMEM],
        out_specs=VMEM,
        out_shape=jax.ShapeDtypeStruct((PACKED[0] + CODE, 2 * CODE), F32),
        compiler_params=SMALL,
        name="codes",
    )(lengths, own, other)


def add_kernel(*refs):
    copies_ref = refs[-1]
    if len(refs) == 3:
        packed = slice(0, PACKED[0])
        total = refs[0][packed] + refs[1][packed]
    else:
        total = refs[0][0]
        for i in range(1, refs[0].shape[0]):
            total = total + refs[0][i]
    for i in range(copies_ref.shape[0]):
        copies_ref[i] = total


def add_and_copy(count, *arrays):
    return pl.pallas_call(
        add_kernel,
        in_specs=[VMEM] * len(arrays),
        out_specs=VMEM,
        out_shape=jax.ShapeDtypeStruct((count,) + PACKED, F32),
        compiler_params=SMALL,
        name="add",
    )(*arrays)


def condition_kernel(parts_ref, own_ref, other_ref, flat_ref, rows_ref, lines_ref):
    packed = parts_ref[0]
    for i in range(1, parts_ref.shape[0]):
        packed = packed + parts_ref[i]
    half = CODE // 2
    square = jnp.concatenate([packed[:half, :CODE], packed[:half, CODE:]], axis=0)
    row = lax.broadcasted_iota(I32, (CODE, CODE), 0)
    col = lax.broadcasted_iota(I32, (CODE, CODE), 1)
    upper = jnp.where(col > row, square, 0.0)
    lower = jnp.where(col < row, square, 0.0)
    diagonal = jnp.where(col == row, square, 0.0)
    trace = jnp.sum(diagonal)
    out_factor = upper + upper.T + diagonal
    in_factor = lower + lower.T + jnp.where(col == row, packed[half : half + 1, :CODE], 0.0)

    row = lax.broadcasted_iota(I32, (CODE, 2 * CODE), 0)
    lane = lax.broadcasted_iota(I32, (CODE, 2 * CODE), 1)
    place = jnp.where(lane < CODE, lane, lane - CODE)
    grid = jnp.concatenate([out_factor, in_factor], axis=1) * (CODE / trace)
    grid = grid + jnp.where(place == row, DAMPING, 0.0)
    for k in range(CODE):
        column = jnp.where(
            lane < CODE, grid[:, k : k + 1], grid[:, CODE + k : CODE + k + 1]
        )
        inverse = 1.0 / column[k : k + 1]
        pivot_row = jnp.where(place[:1] == k, inverse, grid[k : k + 1] * inverse)
        grid = jnp.where(place == k, 0.0, grid) - column * pivot_row
        grid = jnp.where(row == k, pivot_row, grid)

    out_inverse = grid[:, :CODE]
    in_inverse = grid[:, CODE:]
    nn = ((1,), (0,))
    score_scale = 1.0 / math.sqrt(CODE)
    scaled = in_inverse * score_scale
    core = lax.axis_index("cuts")
    mine = pl.ds(pl.multiple_of(core * (half // 2), 8), half // 2)
    for side, ref in enumerate((own_ref, other_ref)):
        left = dot(out_inverse, ref[PACKED[0] :], nn)
        rows_ref[:, :CODE] = dot(left[:, :CODE], scaled, nn)
        rows_ref[:, CODE:] = dot(left[:, CODE:], scaled, nn)
        even = rows_ref[pl.ds(0, half, stride=2), :]
        odd = rows_ref[pl.ds(1, half, stride=2), :]
        lines_ref[:, :CODE] = even[:, :CODE]
        lines_ref[:, CODE:] = odd[:, :CODE]
        flat_ref[2 * side] = lines_ref[mine]
        lines_ref[:, :CODE] = even[:, CODE:]
        lines_ref[:, CODE:] = odd[:, CODE:]
        flat_ref[2 * side + 1] = lines_ref[mine]


def condition(parts, own, other):
    half = CODE // 2
    return pl.pallas_call(
        condition_kernel,
        in_specs=[VMEM] * 3,
        out_specs=VMEM,
        out_shape=jax.ShapeDtypeStruct((4, half // 2, 2 * CODE), F32),
        scratch_shapes=[
            pltpu.VMEM((CODE, 2 * CODE), F32),
            pltpu.VMEM((half, 2 * CODE), F32),
        ],
        compiler_params=SMALL,
        name="condition",
    )(parts, own, other)


def score_kernel(flat_ref, *refs):
    *queries_refs, own_ref, other_ref, sums = refs
    width = 2 * CODE
    depth = flat_ref.shape[1]
    flat = [flat_ref[e] for e in range(4)]
    x = lax.axis_index("x")
    for shift, queries_ref in enumerate(queries_refs):
        count = 2 * queries_ref.shape[0]
        lines = [[], [], [], []]
        for q in range(count):
            first = (q % 2) * depth
            piece = queries_ref[q // 2, first : first + depth].astype(F32)
            for e in range(4):
                product = piece * flat[e]
                lines[e].append(jnp.sum(product, axis=0, keepdims=True))
        came = lax.rem(x + (len(queries_refs) - shift), len(queries_refs))
        place = pl.ds(pl.multiple_of(came * count, count), count)
        for e in range(4):
            sums[e, place] = jnp.concatenate(lines[e], axis=0)
    ones = jnp.ones((8, width), F32)
    for e in range(2):
        own_ref[e : e + 1] = dot(ones, sums[e], ((1,), (1,)))[:1]
        other_ref[e : e + 1] = dot(ones, sums[2 + e], ((1,), (1,)))[:1]


def score(flat, queries):
    count = sum(2 * q.shape[0] for q in queries)
    return pl.pallas_call(
        score_kernel,
        in_specs=[VMEM] * (1 + len(queries)),
        out_specs=[VMEM, VMEM],
        out_shape=[jax.ShapeDtypeStruct((2, count), F32)] * 2,
        scratch_shapes=[pltpu.VMEM((4, count, 2 * CODE), F32)],
        compiler_params=SMALL,
        name="score",
    )(flat, *queries)


SWAP = [(0, 1), (1, 0)]


def on_device(hidden, out_grads, lengths, queries, proj_seeds):
    examples, seq_len, ff_local = hidden.shape
    d_local = out_grads.shape[2]
    own = project(
        proj_seeds, hidden.reshape(-1, ff_local), out_grads.reshape(-1, d_local)
    )
    queries = lax.dynamic_index_in_dim(
        queries.reshape(2, 2, CODE // 4, 2 * CODE), lax.axis_index("cuts"), 1, False
    ).reshape(CODE // 2, 2 * CODE)
    own, queries = lax.optimization_barrier((own, queries))
    other = lax.ppermute(own, "mp", SWAP)
    near = lax.all_to_all(repeat(queries, 32), ("y", "z"), 0, 0)
    other, near = lax.optimization_barrier((other, near))
    made = make_codes(lengths, own, other)
    made_there = lax.ppermute(made, "cuts", SWAP)
    total = add_and_copy(16, made, made_there)
    total, near = lax.optimization_barrier((total, near))
    all_queries = [near]
    for shift in range(1, 4):
        all_queries.append(
            lax.ppermute(near, "x", [(i, (i + shift) % 4) for i in range(4)])
        )
    copies = add_and_copy(8, lax.all_to_all(total, ("x", "y"), 0, 0))
    parts = lax.all_to_all(copies, "z", 0, 0)
    half_here, half_there = score(condition(parts, made, made_there), all_queries)
    return half_here + lax.ppermute(half_there, "cuts", SWAP)


def solution(mesh):
    fine = Mesh(mesh.devices.reshape(2, 4, 4, 8, 2), ("cuts", "x", "y", "z", "mp"))
    rows = ("cuts", "x", "y", "z")
    return jax.shard_map(
        on_device,
        mesh=fine,
        in_specs=(
            P(rows, None, "mp"),
            P(rows, None, "mp"),
            P(rows),
            P(("x", "y", "z"), None),
            P(),
        ),
        out_specs=P(rows, None),
        check_vma=False,
    )
```

```python
import math

import jax
import jax.numpy as jnp
from jax import lax
from jax.experimental import pallas as pl
from jax.experimental.pallas import tpu as pltpu
from jax.sharding import Mesh, PartitionSpec as P

D = 4096
FF = 14336
CODE = 64
DAMPING = 0.1
STEPS = 4
SWAPPED = 768
HIGH = lax.Precision.HIGHEST
F32 = jnp.float32
I32 = jnp.int32
VMEM = pl.BlockSpec(memory_space=pltpu.VMEM)
SMEM = pl.BlockSpec(memory_space=pltpu.SMEM)
PACKED = (CODE // 2 + 8, 2 * CODE)
SMALL = pltpu.CompilerParams(vmem_limit_bytes=4 * 2**20)


def dot(a, b, dims, precision=HIGH):
    return lax.dot_general(
        a, b, (dims, ((), ())), precision=precision, preferred_element_type=F32
    )


def sign_tables(seed, first, second, count):
    lane = lax.broadcasted_iota(I32, (1, 2 * CODE), 1)
    start = jnp.where(lane < CODE, first, second) * 73856093
    rows = lax.broadcasted_iota(I32, (count, 2 * CODE), 0) * 73856093 + start
    hashed = rows ^ ((lane & (CODE - 1)) * 19349663 ^ seed * 83492791)
    hashed = hashed ^ lax.shift_right_logical(hashed, jnp.int32(13))
    hashed = hashed * 1274126177
    hashed = hashed ^ lax.shift_right_logical(hashed, jnp.int32(16))
    return jnp.where((hashed & 128) == 0, 1.0, -1.0).astype(jnp.bfloat16)


def project_kernel(seeds_ref, hidden_ref, grads_ref, part_ref, hidden, grads, table, sems):
    place = lax.axis_index("mp")
    rows, ff_local = hidden_ref.shape
    d_local = grads_ref.shape[1]
    ff_half, d_half = ff_local // 2, d_local // 2
    block = ff_half // STEPS

    def copy(source, held, first, count, i):
        columns = pl.ds(first, count)
        made = pltpu.make_async_copy(source.at[:, columns], held.at[:, columns], sems.at[i])
        made.start()
        return made

    copies = [copy(grads_ref, grads, 0, d_local, 0)]
    for i in range(STEPS):
        copies.append(copy(hidden_ref, hidden, i * block, block, 2 * i + 1))
        copies.append(copy(hidden_ref, hidden, ff_half + i * block, block, 2 * i + 2))
    first = place * d_local
    table[:d_half] = sign_tables(seeds_ref[1], first, first + d_half, d_half)
    for i in range(STEPS):
        first = place * ff_local + i * block
        table[d_half + i * block : d_half + (i + 1) * block] = sign_tables(
            seeds_ref[0], first, first + ff_half, block
        )
    nn = ((1,), (0,))
    copies[0].wait()
    out_left = dot(grads[:, :d_half], table[:d_half], nn, None)
    out_right = dot(grads[:, d_half:], table[:d_half], nn, None)
    in_left = in_right = jnp.zeros((rows, 2 * CODE), F32)
    for i in range(STEPS):
        piece = table[d_half + i * block : d_half + (i + 1) * block]
        copies[2 * i + 1].wait()
        copies[2 * i + 2].wait()
        left = hidden[:, i * block : (i + 1) * block]
        right = hidden[:, ff_half + i * block : ff_half + (i + 1) * block]
        in_left = in_left + dot(left, piece, nn, None)
        in_right = in_right + dot(right, piece, nn, None)
    low = lax.broadcasted_iota(I32, (1, 2 * CODE), 1) < CODE
    out_part = jnp.where(low, out_left, out_right)
    in_part = jnp.where(low, in_left, in_right)
    part_ref[...] = jnp.where(
        low,
        out_part + pltpu.roll(out_part, CODE, 1),
        in_part + pltpu.roll(in_part, CODE, 1),
    )


def project(seeds, hidden, grads):
    hbm = pl.BlockSpec(memory_space=pltpu.HBM)
    depth = (hidden.shape[1] + grads.shape[1]) // 2
    return pl.pallas_call(
        project_kernel,
        in_specs=[SMEM, hbm, hbm],
        out_specs=VMEM,
        out_shape=jax.ShapeDtypeStruct((hidden.shape[0], 2 * CODE), F32),
        scratch_shapes=[
            pltpu.VMEM(hidden.shape, hidden.dtype),
            pltpu.VMEM(grads.shape, grads.dtype),
            pltpu.VMEM((depth, 2 * CODE), jnp.bfloat16),
            pltpu.SemaphoreType.DMA((2 * STEPS + 1,)),
        ],
        compiler_params=pltpu.CompilerParams(vmem_limit_bytes=63 * 2**20),
        name="project",
    )(seeds, hidden, grads)


def codes_kernel(lengths_ref, own_ref, other_ref, made_ref):
    total = own_ref[...] + other_ref[...]
    tokens = total.shape[0] // 2
    position = lax.broadcasted_iota(I32, (tokens, 1), 0)
    codes = []
    for e in range(2):
        length = lengths_ref[e]
        scale = (1.0 / math.sqrt(D)) * (1.0 / math.sqrt(FF))
        weight = jnp.where(position < length, scale / length.astype(F32), 0.0)
        part = total[e * tokens : (e + 1) * tokens]
        both = dot(part * weight, part, ((0,), (0,)))
        codes.append(both[:CODE, CODE:])
    wide = jnp.concatenate(codes, axis=1)
    tall = jnp.concatenate(codes, axis=0)
    made_ref[PACKED[0] : PACKED[0] + CODE] = wide
    out_factor = dot(wide, wide, ((1,), (1,)))
    in_factor = dot(tall, tall, ((0,), (0,)))
    row = lax.broadcasted_iota(I32, (CODE, CODE), 0)
    col = lax.broadcasted_iota(I32, (CODE, CODE), 1)
    square = jnp.where(col >= row, out_factor, in_factor)
    half = CODE // 2
    made_ref[:half] = jnp.concatenate([square[:half], square[half:]], axis=1)
    diagonal = jnp.sum(jnp.where(row == col, in_factor, 0.0), axis=0, keepdims=True)
    tail = jnp.concatenate([diagonal, jnp.zeros_like(diagonal)], axis=1)
    made_ref[half : PACKED[0]] = jnp.broadcast_to(tail, (8, 2 * CODE))


def repeat_kernel(own_ref, queries_ref, near_ref, copies_ref):
    near_ref[...] = own_ref[...]
    core = lax.axis_index("cuts")
    depth = queries_ref.shape[2]
    for q in range(2):
        piece = queries_ref[q, core]
        for i in range(copies_ref.shape[0]):
            copies_ref[i, q * depth : (q + 1) * depth] = piece


def repeat(own, queries, count):
    rows = 2 * queries.shape[2]
    return pl.pallas_call(
        repeat_kernel,
        in_specs=[VMEM, VMEM],
        out_specs=[VMEM, VMEM],
        out_shape=[
            jax.ShapeDtypeStruct(own.shape, own.dtype),
            jax.ShapeDtypeStruct((count, rows, queries.shape[3]), queries.dtype),
        ],
        compiler_params=SMALL,
        cost_estimate=pl.CostEstimate(flops=0, bytes_accessed=2**25, transcendentals=0),
        name="repeat",
    )(own, queries)


def make_codes(lengths, own, other):
    return pl.pallas_call(
        codes_kernel,
        in_specs=[SMEM, VMEM, VMEM],
        out_specs=VMEM,
        out_shape=jax.ShapeDtypeStruct((SWAPPED, 2 * CODE), F32),
        compiler_params=SMALL,
        name="codes",
    )(lengths, own, other)


def add_kernel(*refs):
    copies_ref = refs[-1]
    if len(refs) == 3:
        packed = slice(0, PACKED[0])
        total = refs[0][packed] + refs[1][packed]
    else:
        total = refs[0][0]
        for i in range(1, refs[0].shape[0]):
            total = total + refs[0][i]
    for i in range(copies_ref.shape[0]):
        copies_ref[i] = total


def add_and_copy(count, *arrays):
    return pl.pallas_call(
        add_kernel,
        in_specs=[VMEM] * len(arrays),
        out_specs=VMEM,
        out_shape=jax.ShapeDtypeStruct((count,) + PACKED, F32),
        compiler_params=SMALL,
        name="add",
    )(*arrays)


def invert_both(grid):
    rows = 8
    lane = lax.broadcasted_iota(I32, (rows, 2 * CODE), 1)
    sub = lax.broadcasted_iota(I32, (rows, 2 * CODE), 0)
    place = lane & (CODE - 1)
    first = lane - place

    def column_of(parts, k):
        return [jnp.take_along_axis(part, first + k, axis=1) for part in parts]

    parts = [grid[i : i + rows] for i in range(0, CODE, rows)]
    column = column_of(parts, 0)
    for k in range(CODE):
        at, s = divmod(k, rows)
        inverse = 1.0 / column[at][s : s + 1]
        if k + 1 < CODE:
            later = column_of(parts, k + 1)
            entry = later[at][s : s + 1] * inverse
            later = [new - old * entry for new, old in zip(later, column)]
            later[at] = jnp.where(sub == s, entry, later[at])
        pivot_row = jnp.where(place[:1] == k, inverse, parts[at][s : s + 1] * inverse)
        parts = [
            jnp.where(place == k, 0.0, part) - old * pivot_row
            for part, old in zip(parts, column)
        ]
        parts[at] = jnp.where(sub == s, pivot_row, parts[at])
        column = later
    return jnp.concatenate(parts, axis=0)


def condition_kernel(parts_ref, own_ref, other_ref, flat_ref, rows_ref, lines_ref):
    packed = parts_ref[0]
    for i in range(1, parts_ref.shape[0]):
        packed = packed + parts_ref[i]
    half = CODE // 2
    square = jnp.concatenate([packed[:half, :CODE], packed[:half, CODE:]], axis=0)
    row = lax.broadcasted_iota(I32, (CODE, CODE), 0)
    col = lax.broadcasted_iota(I32, (CODE, CODE), 1)
    upper = jnp.where(col > row, square, 0.0)
    lower = jnp.where(col < row, square, 0.0)
    diagonal = jnp.where(col == row, square, 0.0)
    trace = jnp.sum(diagonal)
    out_factor = upper + upper.T + diagonal
    in_factor = lower + lower.T + jnp.where(col == row, packed[half : half + 1, :CODE], 0.0)

    row = lax.broadcasted_iota(I32, (CODE, 2 * CODE), 0)
    lane = lax.broadcasted_iota(I32, (CODE, 2 * CODE), 1)
    grid = jnp.concatenate([out_factor, in_factor], axis=1) * (CODE / trace)
    grid = grid + jnp.where((lane & (CODE - 1)) == row, DAMPING, 0.0)
    grid = invert_both(grid)
    out_inverse = grid[:, :CODE]
    in_inverse = grid[:, CODE:]
    nn = ((1,), (0,))
    score_scale = 1.0 / math.sqrt(CODE)
    scaled = in_inverse * score_scale
    core = lax.axis_index("cuts")
    mine = pl.ds(pl.multiple_of(core * (half // 2), 8), half // 2)
    for side, ref in enumerate((own_ref, other_ref)):
        left = dot(out_inverse, ref[PACKED[0] : PACKED[0] + CODE], nn)
        rows_ref[:, :CODE] = dot(left[:, :CODE], scaled, nn)
        rows_ref[:, CODE:] = dot(left[:, CODE:], scaled, nn)
        even = rows_ref[pl.ds(0, half, stride=2), :]
        odd = rows_ref[pl.ds(1, half, stride=2), :]
        lines_ref[:, :CODE] = even[:, :CODE]
        lines_ref[:, CODE:] = odd[:, :CODE]
        flat_ref[2 * side] = lines_ref[mine]
        lines_ref[:, :CODE] = even[:, CODE:]
        lines_ref[:, CODE:] = odd[:, CODE:]
        flat_ref[2 * side + 1] = lines_ref[mine]


def condition(parts, own, other):
    half = CODE // 2
    return pl.pallas_call(
        condition_kernel,
        in_specs=[VMEM] * 3,
        out_specs=VMEM,
        out_shape=jax.ShapeDtypeStruct((4, half // 2, 2 * CODE), F32),
        scratch_shapes=[
            pltpu.VMEM((CODE, 2 * CODE), F32),
            pltpu.VMEM((half, 2 * CODE), F32),
        ],
        compiler_params=SMALL,
        name="condition",
    )(parts, own, other)


def score_kernel(flat_ref, *refs):
    *queries_refs, own_ref, other_ref, sums = refs
    width = 2 * CODE
    depth = flat_ref.shape[1]
    flat = [flat_ref[e] for e in range(4)]
    x = lax.axis_index("x")
    for from_x in range(4):
        queries_ref = queries_refs[from_x // 2]
        count = queries_ref.shape[0]
        lines = [[], [], [], []]
        for q in range(count):
            held = (from_x % 2) * (count // 2) + q // 2
            first = (q % 2) * depth
            query = queries_ref[held, first : first + depth].astype(F32)
            for e in range(4):
                lines[e].append(jnp.sum(query * flat[e], axis=0, keepdims=True))
        place = pl.ds(pl.multiple_of((x ^ from_x) * count, count), count)
        for e in range(4):
            sums[e, place] = jnp.concatenate(lines[e], axis=0)
    ones = jnp.ones((8, width), F32)
    for e in range(2):
        own_ref[e : e + 1] = dot(ones, sums[e], ((1,), (1,)))[:1]
        other_ref[e : e + 1] = dot(ones, sums[2 + e], ((1,), (1,)))[:1]


def score(flat, queries):
    count = sum(2 * q.shape[0] for q in queries)
    return pl.pallas_call(
        score_kernel,
        in_specs=[VMEM] * (1 + len(queries)),
        out_specs=[VMEM, VMEM],
        out_shape=[jax.ShapeDtypeStruct((2, count), F32)] * 2,
        scratch_shapes=[pltpu.VMEM((4, count, 2 * CODE), F32)],
        compiler_params=SMALL,
        name="score",
    )(flat, *queries)


SWAP = [(0, 1), (1, 0)]


def on_device(hidden, out_grads, lengths, queries, proj_seeds):
    examples, seq_len, ff_local = hidden.shape
    d_local = out_grads.shape[2]
    own = project(
        proj_seeds, hidden.reshape(-1, ff_local), out_grads.reshape(-1, d_local)
    )
    other = lax.ppermute(own, "mp", SWAP)
    own, queries = lax.optimization_barrier((own, queries))
    own, copies = repeat(own, queries.reshape(2, 2, CODE // 4, 2 * CODE), 32)
    near = lax.all_to_all(copies, ("y", "z"), 0, 0)
    made = make_codes(lengths, own, other)
    made_there = lax.ppermute(made, "cuts", SWAP)
    total = add_and_copy(16, made, made_there)
    total, near = lax.optimization_barrier((total, near))
    pair = [near, lax.ppermute(near, "x", [(i, i ^ 1) for i in range(4)])]
    pair = jnp.concatenate(pair, axis=0)
    all_queries = [pair, lax.ppermute(pair, "x", [(i, i ^ 2) for i in range(4)])]
    copies = add_and_copy(8, lax.all_to_all(total, ("x", "y"), 0, 0))
    parts = lax.all_to_all(copies, "z", 0, 0)
    half_here, half_there = score(condition(parts, made, made_there), all_queries)
    return half_here + lax.ppermute(half_there, "cuts", SWAP)


def solution(mesh):
    fine = Mesh(mesh.devices.reshape(2, 4, 4, 8, 2), ("cuts", "x", "y", "z", "mp"))
    rows = ("cuts", "x", "y", "z")
    return jax.shard_map(
        on_device,
        mesh=fine,
        in_specs=(
            P(rows, None, "mp"),
            P(rows, None, "mp"),
            P(rows),
            P(("x", "y", "z"), None),
            P(),
        ),
        out_specs=P(rows, None),
        check_vma=False,
    )
```

```python
import math

import jax
import jax.numpy as jnp
from jax import lax
from jax.experimental import pallas as pl
from jax.experimental.pallas import tpu as pltpu
from jax.sharding import Mesh, PartitionSpec as P

D = 4096
FF = 14336
CODE = 64
DAMPING = 0.1
STEPS = 4
CODES_FLOPS = 10**10
CONDITION_FLOPS = 10**9
HIGH = lax.Precision.HIGHEST
F32 = jnp.float32
I32 = jnp.int32
VMEM = pl.BlockSpec(memory_space=pltpu.VMEM)
SMEM = pl.BlockSpec(memory_space=pltpu.SMEM)
PACKED = (CODE // 2 + 8, 2 * CODE)
SMALL = pltpu.CompilerParams(vmem_limit_bytes=4 * 2**20)


def dot(a, b, dims, precision=HIGH):
    return lax.dot_general(
        a, b, (dims, ((), ())), precision=precision, preferred_element_type=F32
    )


def sign_tables(seed, first, second, count):
    lane = lax.broadcasted_iota(I32, (1, 2 * CODE), 1)
    start = jnp.where(lane < CODE, first, second) * 73856093
    rows = lax.broadcasted_iota(I32, (count, 2 * CODE), 0) * 73856093 + start
    hashed = rows ^ ((lane & (CODE - 1)) * 19349663 ^ seed * 83492791)
    hashed = hashed ^ lax.shift_right_logical(hashed, jnp.int32(13))
    hashed = hashed * 1274126177
    hashed = hashed ^ lax.shift_right_logical(hashed, jnp.int32(16))
    return jnp.where((hashed & 128) == 0, 1.0, -1.0).astype(jnp.bfloat16)


def project_kernel(
    seeds_ref, queries_ref, hidden_ref, grads_ref, part_ref, copies_ref, hidden, grads, table, sems
):
    place = lax.axis_index("mp")
    rows, ff_local = hidden_ref.shape
    d_local = grads_ref.shape[1]
    ff_half, d_half = ff_local // 2, d_local // 2
    block = ff_half // STEPS

    def copy(source, held, first, count, i):
        columns = pl.ds(first, count)
        made = pltpu.make_async_copy(source.at[:, columns], held.at[:, columns], sems.at[i])
        made.start()
        return made

    copies = [copy(grads_ref, grads, 0, d_local, 0)]
    for i in range(STEPS):
        copies.append(copy(hidden_ref, hidden, i * block, block, 2 * i + 1))
        copies.append(copy(hidden_ref, hidden, ff_half + i * block, block, 2 * i + 2))
    first = place * d_local
    table[:d_half] = sign_tables(seeds_ref[1], first, first + d_half, d_half)
    for i in range(STEPS):
        first = place * ff_local + i * block
        table[d_half + i * block : d_half + (i + 1) * block] = sign_tables(
            seeds_ref[0], first, first + ff_half, block
        )
    width = 2 * CODE
    depth = queries_ref.shape[1] // width // 2
    first = lax.axis_index("cuts") * (depth * width)
    for q in range(2):
        rows_of = [
            queries_ref[q : q + 1, pl.ds(pl.multiple_of(first + j * width, width), width)]
            for j in range(depth)
        ]
        piece = jnp.concatenate([r.astype(F32) for r in rows_of], axis=0).astype(jnp.bfloat16)
        for i in range(copies_ref.shape[0]):
            copies_ref[i, q * depth : (q + 1) * depth] = piece
    nn = ((1,), (0,))
    copies[0].wait()
    out_left = dot(grads[:, :d_half], table[:d_half], nn, None)
    out_right = dot(grads[:, d_half:], table[:d_half], nn, None)
    in_left = in_right = jnp.zeros((rows, 2 * CODE), F32)
    for i in range(STEPS):
        piece = table[d_half + i * block : d_half + (i + 1) * block]
        copies[2 * i + 1].wait()
        copies[2 * i + 2].wait()
        left = hidden[:, i * block : (i + 1) * block]
        right = hidden[:, ff_half + i * block : ff_half + (i + 1) * block]
        in_left = in_left + dot(left, piece, nn, None)
        in_right = in_right + dot(right, piece, nn, None)
    low = lax.broadcasted_iota(I32, (1, 2 * CODE), 1) < CODE
    out_part = jnp.where(low, out_left, out_right)
    in_part = jnp.where(low, in_left, in_right)
    part_ref[...] = jnp.where(
        low,
        out_part + pltpu.roll(out_part, CODE, 1),
        in_part + pltpu.roll(in_part, CODE, 1),
    )


def project(seeds, queries, hidden, grads):
    hbm = pl.BlockSpec(memory_space=pltpu.HBM)
    depth = (hidden.shape[1] + grads.shape[1]) // 2
    return pl.pallas_call(
        project_kernel,
        in_specs=[SMEM, VMEM, hbm, hbm],
        out_specs=[VMEM, VMEM],
        out_shape=[
            jax.ShapeDtypeStruct((hidden.shape[0], 2 * CODE), F32),
            jax.ShapeDtypeStruct((32, CODE // 2, 2 * CODE), queries.dtype),
        ],
        scratch_shapes=[
            pltpu.VMEM(hidden.shape, hidden.dtype),
            pltpu.VMEM(grads.shape, grads.dtype),
            pltpu.VMEM((depth, 2 * CODE), jnp.bfloat16),
            pltpu.SemaphoreType.DMA((2 * STEPS + 1,)),
        ],
        compiler_params=pltpu.CompilerParams(vmem_limit_bytes=127 * 2**19),
        name="project",
    )(seeds, queries, hidden, grads)


def codes_kernel(lengths_ref, own_ref, other_ref, made_ref, held, sem):
    copy = pltpu.make_async_copy(own_ref, held, sem)
    copy.start()
    copy.wait()
    total = held[...] + other_ref[...]
    tokens = total.shape[0] // 2
    position = lax.broadcasted_iota(I32, (tokens, 1), 0)
    codes = []
    for e in range(2):
        length = lengths_ref[e]
        scale = (1.0 / math.sqrt(D)) * (1.0 / math.sqrt(FF))
        weight = jnp.where(position < length, scale / length.astype(F32), 0.0)
        part = total[e * tokens : (e + 1) * tokens]
        both = dot(part * weight, part, ((0,), (0,)))
        codes.append(both[:CODE, CODE:])
    wide = jnp.concatenate(codes, axis=1)
    tall = jnp.concatenate(codes, axis=0)
    made_ref[PACKED[0] : PACKED[0] + CODE] = wide
    out_factor = dot(wide, wide, ((1,), (1,)))
    in_factor = dot(tall, tall, ((0,), (0,)))
    row = lax.broadcasted_iota(I32, (CODE, CODE), 0)
    col = lax.broadcasted_iota(I32, (CODE, CODE), 1)
    square = jnp.where(col >= row, out_factor, in_factor)
    half = CODE // 2
    made_ref[:half] = jnp.concatenate([square[:half], square[half:]], axis=1)
    diagonal = jnp.sum(jnp.where(row == col, in_factor, 0.0), axis=0, keepdims=True)
    tail = jnp.concatenate([diagonal, jnp.zeros_like(diagonal)], axis=1)
    made_ref[half : PACKED[0]] = jnp.broadcast_to(tail, (8, 2 * CODE))


def make_codes(lengths, own, other):
    return pl.pallas_call(
        codes_kernel,
        in_specs=[SMEM, pl.BlockSpec(memory_space=pltpu.HBM), VMEM],
        out_specs=VMEM,
        out_shape=jax.ShapeDtypeStruct((PACKED[0] + CODE, 2 * CODE), F32),
        scratch_shapes=[pltpu.VMEM(own.shape, own.dtype), pltpu.SemaphoreType.DMA],
        compiler_params=SMALL,
        cost_estimate=pl.CostEstimate(flops=CODES_FLOPS, bytes_accessed=0, transcendentals=0),
        name="codes",
    )(lengths, own, other)


def add_kernel(*refs):
    copies_ref = refs[-1]
    if len(refs) == 3:
        packed = slice(0, PACKED[0])
        total = refs[0][packed] + refs[1][packed]
    else:
        total = refs[0][0]
        for i in range(1, refs[0].shape[0]):
            total = total + refs[0][i]
    for i in range(copies_ref.shape[0]):
        copies_ref[i] = total


def add_and_copy(count, *arrays):
    return pl.pallas_call(
        add_kernel,
        in_specs=[VMEM] * len(arrays),
        out_specs=VMEM,
        out_shape=jax.ShapeDtypeStruct((count,) + PACKED, F32),
        compiler_params=SMALL,
        name="add",
    )(*arrays)


def invert_both(grid):
    rows = 8
    lane = lax.broadcasted_iota(I32, (rows, 2 * CODE), 1)
    sub = lax.broadcasted_iota(I32, (rows, 2 * CODE), 0)
    place = lane & (CODE - 1)
    first = lane - place

    def columns_of(parts, k):
        return [
            [jnp.take_along_axis(part, first + (k + i), axis=1) for part in parts]
            for i in range(2)
        ]

    parts = [grid[i : i + rows] for i in range(0, CODE, rows)]
    left, right = columns_of(parts, 0)
    for k in range(0, CODE, 2):
        at, s = divmod(k, rows)
        a, b = left[at][s : s + 1], right[at][s : s + 1]
        c, d = left[at][s + 1 : s + 2], right[at][s + 1 : s + 2]
        scale = 1.0 / (a * d - b * c)
        a, b, c, d = d * scale, -b * scale, -c * scale, a * scale

        def pivot_rows(parts):
            one, two = parts[at][s : s + 1], parts[at][s + 1 : s + 2]
            return a * one + b * two, c * one + d * two

        def update(parts, one, two):
            parts = [p - l * one - r * two for p, l, r in zip(parts, left, right)]
            parts[at] = jnp.where(sub == s, one, jnp.where(sub == s + 1, two, parts[at]))
            return parts

        if k + 2 < CODE:
            later = [update(new, *pivot_rows(new)) for new in columns_of(parts, k + 2)]
        one, two = pivot_rows(parts)
        one = jnp.where(place[:1] == k, a, jnp.where(place[:1] == k + 1, b, one))
        two = jnp.where(place[:1] == k, c, jnp.where(place[:1] == k + 1, d, two))
        here = (place == k) | (place == k + 1)
        parts = update([jnp.where(here, 0.0, part) for part in parts], one, two)
        left, right = later
    return jnp.concatenate(parts, axis=0)


def condition_kernel(parts_ref, own_ref, other_ref, flat_ref, rows_ref, lines_ref):
    packed = parts_ref[0]
    for i in range(1, parts_ref.shape[0]):
        packed = packed + parts_ref[i]
    half = CODE // 2
    square = jnp.concatenate([packed[:half, :CODE], packed[:half, CODE:]], axis=0)
    row = lax.broadcasted_iota(I32, (CODE, CODE), 0)
    col = lax.broadcasted_iota(I32, (CODE, CODE), 1)
    upper = jnp.where(col > row, square, 0.0)
    lower = jnp.where(col < row, square, 0.0)
    diagonal = jnp.where(col == row, square, 0.0)
    trace = jnp.sum(diagonal)
    out_factor = upper + upper.T + diagonal
    in_factor = lower + lower.T + jnp.where(col == row, packed[half : half + 1, :CODE], 0.0)

    row = lax.broadcasted_iota(I32, (CODE, 2 * CODE), 0)
    lane = lax.broadcasted_iota(I32, (CODE, 2 * CODE), 1)
    grid = jnp.concatenate([out_factor, in_factor], axis=1) * (CODE / trace)
    grid = grid + jnp.where((lane & (CODE - 1)) == row, DAMPING, 0.0)
    grid = invert_both(grid)
    out_inverse = grid[:, :CODE]
    in_inverse = grid[:, CODE:]
    nn = ((1,), (0,))
    score_scale = 1.0 / math.sqrt(CODE)
    scaled = in_inverse * score_scale
    core = lax.axis_index("cuts")
    mine = pl.ds(pl.multiple_of(core * (half // 2), 8), half // 2)
    for side, ref in enumerate((own_ref, other_ref)):
        left = dot(out_inverse, ref[PACKED[0] : PACKED[0] + CODE], nn)
        rows_ref[:, :CODE] = dot(left[:, :CODE], scaled, nn)
        rows_ref[:, CODE:] = dot(left[:, CODE:], scaled, nn)
        even = rows_ref[pl.ds(0, half, stride=2), :]
        odd = rows_ref[pl.ds(1, half, stride=2), :]
        lines_ref[:, :CODE] = even[:, :CODE]
        lines_ref[:, CODE:] = odd[:, :CODE]
        flat_ref[2 * side] = lines_ref[mine]
        lines_ref[:, :CODE] = even[:, CODE:]
        lines_ref[:, CODE:] = odd[:, CODE:]
        flat_ref[2 * side + 1] = lines_ref[mine]


def condition(parts, own, other):
    half = CODE // 2
    return pl.pallas_call(
        condition_kernel,
        in_specs=[VMEM] * 3,
        out_specs=VMEM,
        out_shape=jax.ShapeDtypeStruct((4, half // 2, 2 * CODE), F32),
        scratch_shapes=[
            pltpu.VMEM((CODE, 2 * CODE), F32),
            pltpu.VMEM((half, 2 * CODE), F32),
        ],
        compiler_params=SMALL,
        cost_estimate=pl.CostEstimate(flops=CONDITION_FLOPS, bytes_accessed=0, transcendentals=0),
        name="condition",
    )(parts, own, other)


def row_sums(arrays):
    sub = lax.broadcasted_iota(I32, (8, 2 * CODE), 0)
    for shift in (1, 2, 4):
        low = (sub & shift) == 0
        arrays = [
            jnp.where(low, a, b) + pltpu.roll(jnp.where(low, b, a), shift, 0)
            for a, b in zip(arrays[::2], arrays[1::2])
        ]
    return arrays[0]


def score_kernel(flat_ref, *refs):
    *queries_refs, own_ref, other_ref, sums = refs
    width = 2 * CODE
    depth = flat_ref.shape[1]
    flat = [flat_ref[e] for e in range(4)]
    x = lax.axis_index("x")
    places = len(queries_refs)
    for behind, queries_ref in enumerate(queries_refs):
        count = 2 * queries_ref.shape[0]
        came = lax.rem(x + (places - behind), places) * count
        for group in range(0, count, 8):
            products = [[], [], [], []]
            for q in range(group, group + 8):
                first = (q % 2) * depth
                query = queries_ref[q // 2, first : first + depth].astype(F32)
                for e in range(4):
                    product = query * flat[e]
                    products[e].append(product[: depth // 2] + product[depth // 2 :])
            place = pl.ds(pl.multiple_of(came + group, 8), 8)
            for e in range(4):
                sums[e, place] = row_sums(products[e])
    ones = jnp.ones((8, width), F32)
    for e in range(2):
        own_ref[e : e + 1] = dot(ones, sums[e], ((1,), (1,)))[:1]
        other_ref[e : e + 1] = dot(ones, sums[2 + e], ((1,), (1,)))[:1]


def score(flat, queries):
    count = sum(2 * q.shape[0] for q in queries)
    return pl.pallas_call(
        score_kernel,
        in_specs=[VMEM] * (1 + len(queries)),
        out_specs=[VMEM, VMEM],
        out_shape=[jax.ShapeDtypeStruct((2, count), F32)] * 2,
        scratch_shapes=[pltpu.VMEM((4, count, 2 * CODE), F32)],
        compiler_params=SMALL,
        name="score",
    )(flat, *queries)


def join_kernel(here_ref, there_ref, out_ref):
    out_ref[...] = here_ref[...] + there_ref[...]


def join(here, there):
    return pl.pallas_call(
        join_kernel,
        in_specs=[VMEM, VMEM],
        out_specs=VMEM,
        out_shape=jax.ShapeDtypeStruct(here.shape, F32),
        compiler_params=SMALL,
        name="join",
    )(here, there)


SWAP = [(0, 1), (1, 0)]


def on_device(hidden, out_grads, lengths, queries, proj_seeds):
    examples, seq_len, ff_local = hidden.shape
    d_local = out_grads.shape[2]
    own, copies = project(
        proj_seeds, queries, hidden.reshape(-1, ff_local), out_grads.reshape(-1, d_local)
    )
    other = lax.ppermute(own, "mp", SWAP)
    near = lax.all_to_all(copies, ("y", "z"), 0, 0)
    made = make_codes(lengths, own, other)
    made_there = lax.ppermute(made, "cuts", SWAP)
    total = add_and_copy(16, made, made_there)
    total, near = lax.optimization_barrier((total, near))
    up = [(i, (i + 1) % 4) for i in range(4)]
    down = [(i, (i + 3) % 4) for i in range(4)]
    from_below = lax.ppermute(near, "x", up)
    from_above = lax.ppermute(near, "x", down)
    from_across = lax.ppermute(from_below, "x", up)
    all_queries = [near, from_below, from_across, from_above]
    copies = add_and_copy(8, lax.all_to_all(total, ("x", "y"), 0, 0))
    parts = lax.all_to_all(copies, "z", 0, 0)
    half_here, half_there = score(condition(parts, made, made_there), all_queries)
    return join(half_here, lax.ppermute(half_there, "cuts", SWAP))


def solution(mesh):
    fine = Mesh(mesh.devices.reshape(2, 4, 4, 8, 2), ("cuts", "x", "y", "z", "mp"))
    rows = ("cuts", "x", "y", "z")
    return jax.shard_map(
        on_device,
        mesh=fine,
        in_specs=(
            P(rows, None, "mp"),
            P(rows, None, "mp"),
            P(rows),
            P(("x", "y", "z"), None),
            P(),
        ),
        out_specs=P(rows, None),
        check_vma=False,
    )
```

```python
import math

import jax
import jax.numpy as jnp
from jax import lax
from jax.experimental import pallas as pl
from jax.experimental.pallas import tpu as pltpu
from jax.sharding import Mesh, PartitionSpec as P

D = 4096
FF = 14336
CODE = 64
DAMPING = 0.1
STEPS = 4
CODES_FLOPS = 10**10
CONDITION_FLOPS = 10**9
HOLD_FLOPS = 10**9
HIGH = lax.Precision.HIGHEST
F32 = jnp.float32
I32 = jnp.int32
VMEM = pl.BlockSpec(memory_space=pltpu.VMEM)
SMEM = pl.BlockSpec(memory_space=pltpu.SMEM)
PACKED = (CODE // 2 + 8, 2 * CODE)
SMALL = pltpu.CompilerParams(vmem_limit_bytes=4 * 2**20)


def dot(a, b, dims, precision=HIGH):
    return lax.dot_general(
        a, b, (dims, ((), ())), precision=precision, preferred_element_type=F32
    )


def write_tables(table, seed, first, second):
    block = 256
    lane = lax.broadcasted_iota(I32, (1, 2 * CODE), 1)
    start = jnp.where(lane < CODE, first, second) * 73856093
    rows = lax.broadcasted_iota(I32, (block, 2 * CODE), 0) * 73856093 + start
    mixed = (lane & (CODE - 1)) * 19349663 ^ seed * 83492791
    for i in range(0, table.shape[0], block):
        count = min(block, table.shape[0] - i)
        step = (i * 73856093 + 2**31) % 2**32 - 2**31
        hashed = (rows[:count] + jnp.int32(step)) ^ mixed
        hashed = hashed ^ lax.shift_right_logical(hashed, jnp.int32(13))
        hashed = hashed * 1274126177
        hashed = hashed ^ lax.shift_right_logical(hashed, jnp.int32(16))
        signs = jnp.where((hashed & 128) == 0, 1.0, -1.0)
        table[i : i + count] = signs.astype(jnp.bfloat16)


def project_kernel(
    seeds_ref, queries_ref, hidden_ref, grads_ref, part_ref, copies_ref, hidden, grads, table, sems
):
    place = lax.axis_index("mp")
    rows, ff_local = hidden_ref.shape
    d_local = grads_ref.shape[1]
    ff_half, d_half = ff_local // 2, d_local // 2
    block = ff_half // STEPS

    def copy(source, held, first, count, i):
        columns = pl.ds(first, count)
        made = pltpu.make_async_copy(source.at[:, columns], held.at[:, columns], sems.at[i])
        made.start()
        return made

    copies = [copy(grads_ref, grads, 0, d_local, 0)]
    for i in range(STEPS):
        copies.append(copy(hidden_ref, hidden, i * block, block, 2 * i + 1))
        copies.append(copy(hidden_ref, hidden, ff_half + i * block, block, 2 * i + 2))
    first = place * d_local
    write_tables(table.at[:d_half], seeds_ref[1], first, first + d_half)
    first = place * ff_local
    write_tables(table.at[d_half:], seeds_ref[0], first, first + ff_half)
    width = 2 * CODE
    depth = queries_ref.shape[1] // width // 2
    first = lax.axis_index("cuts") * (depth * width)
    for q in range(2):
        rows_of = [
            queries_ref[q : q + 1, pl.ds(pl.multiple_of(first + j * width, width), width)]
            for j in range(depth)
        ]
        piece = jnp.concatenate([r.astype(F32) for r in rows_of], axis=0).astype(jnp.bfloat16)
        for i in range(copies_ref.shape[0]):
            copies_ref[i, q * depth : (q + 1) * depth] = piece
    nn = ((1,), (0,))
    copies[0].wait()
    out_left = dot(grads[:, :d_half], table[:d_half], nn, None)
    out_right = dot(grads[:, d_half:], table[:d_half], nn, None)
    in_left = in_right = jnp.zeros((rows, 2 * CODE), F32)
    for i in range(STEPS):
        piece = table[d_half + i * block : d_half + (i + 1) * block]
        copies[2 * i + 1].wait()
        copies[2 * i + 2].wait()
        left = hidden[:, i * block : (i + 1) * block]
        right = hidden[:, ff_half + i * block : ff_half + (i + 1) * block]
        in_left = in_left + dot(left, piece, nn, None)
        in_right = in_right + dot(right, piece, nn, None)
    low = lax.broadcasted_iota(I32, (1, 2 * CODE), 1) < CODE
    out_part = jnp.where(low, out_left, out_right)
    in_part = jnp.where(low, in_left, in_right)
    part_ref[...] = jnp.where(
        low,
        out_part + pltpu.roll(out_part, CODE, 1),
        in_part + pltpu.roll(in_part, CODE, 1),
    )


def project(seeds, queries, hidden, grads):
    hbm = pl.BlockSpec(memory_space=pltpu.HBM)
    depth = (hidden.shape[1] + grads.shape[1]) // 2
    return pl.pallas_call(
        project_kernel,
        in_specs=[SMEM, VMEM, hbm, hbm],
        out_specs=[VMEM, VMEM],
        out_shape=[
            jax.ShapeDtypeStruct((hidden.shape[0], 2 * CODE), F32),
            jax.ShapeDtypeStruct((32, CODE // 2, 2 * CODE), queries.dtype),
        ],
        scratch_shapes=[
            pltpu.VMEM(hidden.shape, hidden.dtype),
            pltpu.VMEM(grads.shape, grads.dtype),
            pltpu.VMEM((depth, 2 * CODE), jnp.bfloat16),
            pltpu.SemaphoreType.DMA((2 * STEPS + 1,)),
        ],
        compiler_params=pltpu.CompilerParams(vmem_limit_bytes=127 * 2**19),
        name="project",
    )(seeds, queries, hidden, grads)


def codes_kernel(lengths_ref, own_ref, other_ref, made_ref):
    total = own_ref[...] + other_ref[...]
    tokens = total.shape[0] // 2
    position = lax.broadcasted_iota(I32, (tokens, 1), 0)
    codes = []
    for e in range(2):
        length = lengths_ref[e]
        scale = (1.0 / math.sqrt(D)) * (1.0 / math.sqrt(FF))
        weight = jnp.where(position < length, scale / length.astype(F32), 0.0)
        part = total[e * tokens : (e + 1) * tokens]
        both = dot(part * weight, part, ((0,), (0,)))
        codes.append(both[:CODE, CODE:])
    wide = jnp.concatenate(codes, axis=1)
    tall = jnp.concatenate(codes, axis=0)
    made_ref[PACKED[0] : PACKED[0] + CODE] = wide
    out_factor = dot(wide, wide, ((1,), (1,)))
    in_factor = dot(tall, tall, ((0,), (0,)))
    row = lax.broadcasted_iota(I32, (CODE, CODE), 0)
    col = lax.broadcasted_iota(I32, (CODE, CODE), 1)
    square = jnp.where(col >= row, out_factor, in_factor)
    half = CODE // 2
    made_ref[:half] = jnp.concatenate([square[:half], square[half:]], axis=1)
    diagonal = jnp.sum(jnp.where(row == col, in_factor, 0.0), axis=0, keepdims=True)
    tail = jnp.concatenate([diagonal, jnp.zeros_like(diagonal)], axis=1)
    made_ref[half : PACKED[0]] = jnp.broadcast_to(tail, (8, 2 * CODE))


def hold_kernel(own_ref, held_ref):
    held_ref[...] = own_ref[...]


def hold(own):
    return pl.pallas_call(
        hold_kernel,
        in_specs=[VMEM],
        out_specs=VMEM,
        out_shape=jax.ShapeDtypeStruct(own.shape, own.dtype),
        compiler_params=SMALL,
        cost_estimate=pl.CostEstimate(flops=HOLD_FLOPS, bytes_accessed=0, transcendentals=0),
        name="hold",
    )(own)


def make_codes(lengths, own, other):
    return pl.pallas_call(
        codes_kernel,
        in_specs=[SMEM, VMEM, VMEM],
        out_specs=VMEM,
        out_shape=jax.ShapeDtypeStruct((PACKED[0] + CODE, 2 * CODE), F32),
        compiler_params=SMALL,
        cost_estimate=pl.CostEstimate(flops=CODES_FLOPS, bytes_accessed=0, transcendentals=0),
        name="codes",
    )(lengths, own, other)


def add_kernel(*refs):
    copies_ref = refs[-1]
    if len(refs) == 3:
        packed = slice(0, PACKED[0])
        total = refs[0][packed] + refs[1][packed]
    else:
        total = refs[0][0]
        for i in range(1, refs[0].shape[0]):
            total = total + refs[0][i]
    for i in range(copies_ref.shape[0]):
        copies_ref[i] = total


def add_and_copy(count, *arrays):
    return pl.pallas_call(
        add_kernel,
        in_specs=[VMEM] * len(arrays),
        out_specs=VMEM,
        out_shape=jax.ShapeDtypeStruct((count,) + PACKED, F32),
        compiler_params=SMALL,
        name="add",
    )(*arrays)


def invert_both(grid):
    rows = 8
    lane = lax.broadcasted_iota(I32, (rows, 2 * CODE), 1)
    sub = lax.broadcasted_iota(I32, (rows, 2 * CODE), 0)
    place = lane & (CODE - 1)
    first = lane - place

    def columns_of(parts, k):
        return [
            [jnp.take_along_axis(part, first + (k + i), axis=1) for part in parts]
            for i in range(2)
        ]

    parts = [grid[i : i + rows] for i in range(0, CODE, rows)]
    left, right = columns_of(parts, 0)
    for k in range(0, CODE, 2):
        at, s = divmod(k, rows)
        a, b = left[at][s : s + 1], right[at][s : s + 1]
        c, d = left[at][s + 1 : s + 2], right[at][s + 1 : s + 2]
        scale = 1.0 / (a * d - b * c)
        a, b, c, d = d * scale, -b * scale, -c * scale, a * scale

        def pivot_rows(parts):
            one, two = parts[at][s : s + 1], parts[at][s + 1 : s + 2]
            return a * one + b * two, c * one + d * two

        def update(parts, one, two):
            parts = [p - l * one - r * two for p, l, r in zip(parts, left, right)]
            parts[at] = jnp.where(sub == s, one, jnp.where(sub == s + 1, two, parts[at]))
            return parts

        if k + 2 < CODE:
            later = [update(new, *pivot_rows(new)) for new in columns_of(parts, k + 2)]
        one, two = pivot_rows(parts)
        one = jnp.where(place[:1] == k, a, jnp.where(place[:1] == k + 1, b, one))
        two = jnp.where(place[:1] == k, c, jnp.where(place[:1] == k + 1, d, two))
        here = (place == k) | (place == k + 1)
        parts = update([jnp.where(here, 0.0, part) for part in parts], one, two)
        left, right = later
    return jnp.concatenate(parts, axis=0)


def condition_kernel(parts_ref, own_ref, other_ref, flat_ref, rows_ref, lines_ref):
    packed = parts_ref[0]
    for i in range(1, parts_ref.shape[0]):
        packed = packed + parts_ref[i]
    half = CODE // 2
    square = jnp.concatenate([packed[:half, :CODE], packed[:half, CODE:]], axis=0)
    row = lax.broadcasted_iota(I32, (CODE, CODE), 0)
    col = lax.broadcasted_iota(I32, (CODE, CODE), 1)
    upper = jnp.where(col > row, square, 0.0)
    lower = jnp.where(col < row, square, 0.0)
    diagonal = jnp.where(col == row, square, 0.0)
    trace = jnp.sum(diagonal)
    out_factor = upper + upper.T + diagonal
    in_factor = lower + lower.T + jnp.where(col == row, packed[half : half + 1, :CODE], 0.0)

    row = lax.broadcasted_iota(I32, (CODE, 2 * CODE), 0)
    lane = lax.broadcasted_iota(I32, (CODE, 2 * CODE), 1)
    grid = jnp.concatenate([out_factor, in_factor], axis=1) * (CODE / trace)
    grid = grid + jnp.where((lane & (CODE - 1)) == row, DAMPING, 0.0)
    grid = invert_both(grid)
    out_inverse = grid[:, :CODE]
    in_inverse = grid[:, CODE:]
    nn = ((1,), (0,))
    score_scale = 1.0 / math.sqrt(CODE)
    scaled = in_inverse * score_scale
    core = lax.axis_index("cuts")
    mine = pl.ds(pl.multiple_of(core * (half // 2), 8), half // 2)
    for side, ref in enumerate((own_ref, other_ref)):
        left = dot(out_inverse, ref[PACKED[0] : PACKED[0] + CODE], nn)
        rows_ref[:, :CODE] = dot(left[:, :CODE], scaled, nn)
        rows_ref[:, CODE:] = dot(left[:, CODE:], scaled, nn)
        even = rows_ref[pl.ds(0, half, stride=2), :]
        odd = rows_ref[pl.ds(1, half, stride=2), :]
        lines_ref[:, :CODE] = even[:, :CODE]
        lines_ref[:, CODE:] = odd[:, :CODE]
        flat_ref[2 * side] = lines_ref[mine]
        lines_ref[:, :CODE] = even[:, CODE:]
        lines_ref[:, CODE:] = odd[:, CODE:]
        flat_ref[2 * side + 1] = lines_ref[mine]


def condition(parts, own, other):
    half = CODE // 2
    return pl.pallas_call(
        condition_kernel,
        in_specs=[VMEM] * 3,
        out_specs=VMEM,
        out_shape=jax.ShapeDtypeStruct((4, half // 2, 2 * CODE), F32),
        scratch_shapes=[
            pltpu.VMEM((CODE, 2 * CODE), F32),
            pltpu.VMEM((half, 2 * CODE), F32),
        ],
        compiler_params=SMALL,
        cost_estimate=pl.CostEstimate(flops=CONDITION_FLOPS, bytes_accessed=0, transcendentals=0),
        name="condition",
    )(parts, own, other)


def row_sums(arrays):
    sub = lax.broadcasted_iota(I32, (8, 2 * CODE), 0)
    for shift in (1, 2, 4):
        low = (sub & shift) == 0
        arrays = [
            jnp.where(low, a, b) + pltpu.roll(jnp.where(low, b, a), shift, 0)
            for a, b in zip(arrays[::2], arrays[1::2])
        ]
    return arrays[0]


def score_kernel(flat_ref, *refs):
    *queries_refs, own_ref, other_ref, sums = refs
    width = 2 * CODE
    depth = flat_ref.shape[1]
    flat = [flat_ref[e] for e in range(4)]
    x = lax.axis_index("x")
    places = len(queries_refs)
    for behind, queries_ref in enumerate(queries_refs):
        count = 2 * queries_ref.shape[0]
        came = lax.rem(x + (places - behind), places) * count
        for group in range(0, count, 8):
            products = [[], [], [], []]
            for q in range(group, group + 8):
                first = (q % 2) * depth
                query = queries_ref[q // 2, first : first + depth].astype(F32)
                for e in range(4):
                    product = query * flat[e]
                    products[e].append(product[: depth // 2] + product[depth // 2 :])
            place = pl.ds(pl.multiple_of(came + group, 8), 8)
            for e in range(4):
                sums[e, place] = row_sums(products[e])
    ones = jnp.ones((8, width), F32)
    for e in range(2):
        own_ref[e : e + 1] = dot(ones, sums[e], ((1,), (1,)))[:1]
        other_ref[e : e + 1] = dot(ones, sums[2 + e], ((1,), (1,)))[:1]


def score(flat, queries):
    count = sum(2 * q.shape[0] for q in queries)
    return pl.pallas_call(
        score_kernel,
        in_specs=[VMEM] * (1 + len(queries)),
        out_specs=[VMEM, VMEM],
        out_shape=[jax.ShapeDtypeStruct((2, count), F32)] * 2,
        scratch_shapes=[pltpu.VMEM((4, count, 2 * CODE), F32)],
        compiler_params=SMALL,
        name="score",
    )(flat, *queries)


def join_kernel(here_ref, there_ref, out_ref):
    out_ref[...] = here_ref[...] + there_ref[...]


def join(here, there):
    return pl.pallas_call(
        join_kernel,
        in_specs=[VMEM, VMEM],
        out_specs=VMEM,
        out_shape=jax.ShapeDtypeStruct(here.shape, F32),
        compiler_params=SMALL,
        name="join",
    )(here, there)


SWAP = [(0, 1), (1, 0)]


def on_device(hidden, out_grads, lengths, queries, proj_seeds):
    examples, seq_len, ff_local = hidden.shape
    d_local = out_grads.shape[2]
    own, copies = project(
        proj_seeds, queries, hidden.reshape(-1, ff_local), out_grads.reshape(-1, d_local)
    )
    other = lax.ppermute(own, "mp", SWAP)
    near = lax.all_to_all(copies, ("y", "z"), 0, 0)
    made = make_codes(lengths, hold(own), other)
    made_there = lax.ppermute(made, "cuts", SWAP)
    total = add_and_copy(16, made, made_there)
    total, near = lax.optimization_barrier((total, near))
    up = [(i, (i + 1) % 4) for i in range(4)]
    down = [(i, (i + 3) % 4) for i in range(4)]
    from_below = lax.ppermute(near, "x", up)
    from_above = lax.ppermute(near, "x", down)
    from_below, from_above = lax.optimization_barrier((from_below, from_above))
    from_across = lax.ppermute(from_below, "x", up)
    all_queries = [near, from_below, from_across, from_above]
    copies = add_and_copy(8, lax.all_to_all(total, ("x", "y"), 0, 0))
    parts = lax.all_to_all(copies, "z", 0, 0)
    half_here, half_there = score(condition(parts, made, made_there), all_queries)
    return join(half_here, lax.ppermute(half_there, "cuts", SWAP))


def solution(mesh):
    fine = Mesh(mesh.devices.reshape(2, 4, 4, 8, 2), ("cuts", "x", "y", "z", "mp"))
    rows = ("cuts", "x", "y", "z")
    return jax.shard_map(
        on_device,
        mesh=fine,
        in_specs=(
            P(rows, None, "mp"),
            P(rows, None, "mp"),
            P(rows),
            P(("x", "y", "z"), None),
            P(),
        ),
        out_specs=P(rows, None),
        check_vma=False,
    )
```

```python
import math

import jax
import jax.numpy as jnp
from jax import lax
from jax.experimental import pallas as pl
from jax.experimental.pallas import tpu as pltpu
from jax.sharding import Mesh, PartitionSpec as P

D = 4096
FF = 14336
CODE = 64
DAMPING = 0.1
STEPS = 4
CODES_FLOPS = 10**10
CONDITION_FLOPS = 10**9
HOLD_FLOPS = 10**9
HIGH = lax.Precision.HIGHEST
F32 = jnp.float32
I32 = jnp.int32
VMEM = pl.BlockSpec(memory_space=pltpu.VMEM)
SMEM = pl.BlockSpec(memory_space=pltpu.SMEM)
PACKED = (CODE // 2 + 8, 2 * CODE)
SMALL = pltpu.CompilerParams(vmem_limit_bytes=4 * 2**20)


def dot(a, b, dims, precision=HIGH):
    return lax.dot_general(
        a, b, (dims, ((), ())), precision=precision, preferred_element_type=F32
    )


def write_tables(table, seed, first, second):
    block = 256
    lane = lax.broadcasted_iota(I32, (1, 2 * CODE), 1)
    start = jnp.where(lane < CODE, first, second) * 73856093
    rows = lax.broadcasted_iota(I32, (block, 2 * CODE), 0) * 73856093 + start
    mixed = (lane & (CODE - 1)) * 19349663 ^ seed * 83492791
    for i in range(0, table.shape[0], block):
        count = min(block, table.shape[0] - i)
        step = (i * 73856093 + 2**31) % 2**32 - 2**31
        hashed = (rows[:count] + jnp.int32(step)) ^ mixed
        hashed = hashed ^ lax.shift_right_logical(hashed, jnp.int32(13))
        hashed = hashed * 1274126177
        hashed = hashed ^ lax.shift_right_logical(hashed, jnp.int32(16))
        signs = jnp.where((hashed & 128) == 0, 1.0, -1.0)
        table[i : i + count] = signs.astype(jnp.bfloat16)


def project_kernel(
    seeds_ref, queries_ref, hidden_ref, grads_ref, part_ref, copies_ref, hidden, grads, table, sems
):
    place = lax.axis_index("mp")
    rows, ff_local = hidden_ref.shape
    d_local = grads_ref.shape[1]
    ff_half, d_half = ff_local // 2, d_local // 2
    block = ff_half // STEPS

    def copy(source, held, first, count, i):
        columns = pl.ds(first, count)
        made = pltpu.make_async_copy(source.at[:, columns], held.at[:, columns], sems.at[i])
        made.start()
        return made

    copies = [copy(grads_ref, grads, 0, d_local, 0)]
    for i in range(STEPS):
        copies.append(copy(hidden_ref, hidden, i * block, block, 2 * i + 1))
        copies.append(copy(hidden_ref, hidden, ff_half + i * block, block, 2 * i + 2))
    first = place * d_local
    write_tables(table.at[:d_half], seeds_ref[1], first, first + d_half)
    first = place * ff_local
    write_tables(table.at[d_half:], seeds_ref[0], first, first + ff_half)
    width = 2 * CODE
    depth = queries_ref.shape[1] // width // 2
    first = lax.axis_index("cuts") * (depth * width)
    for q in range(2):
        rows_of = [
            queries_ref[q : q + 1, pl.ds(pl.multiple_of(first + j * width, width), width)]
            for j in range(depth)
        ]
        piece = jnp.concatenate([r.astype(F32) for r in rows_of], axis=0).astype(jnp.bfloat16)
        for i in range(copies_ref.shape[0]):
            copies_ref[i, q * depth : (q + 1) * depth] = piece
    nn = ((1,), (0,))
    copies[0].wait()
    out_left = dot(grads[:, :d_half], table[:d_half], nn, None)
    out_right = dot(grads[:, d_half:], table[:d_half], nn, None)
    in_left = in_right = jnp.zeros((rows, 2 * CODE), F32)
    for i in range(STEPS):
        piece = table[d_half + i * block : d_half + (i + 1) * block]
        copies[2 * i + 1].wait()
        copies[2 * i + 2].wait()
        left = hidden[:, i * block : (i + 1) * block]
        right = hidden[:, ff_half + i * block : ff_half + (i + 1) * block]
        in_left = in_left + dot(left, piece, nn, None)
        in_right = in_right + dot(right, piece, nn, None)
    low = lax.broadcasted_iota(I32, (1, 2 * CODE), 1) < CODE
    out_part = jnp.where(low, out_left, out_right)
    in_part = jnp.where(low, in_left, in_right)
    part_ref[...] = jnp.where(
        low,
        out_part + pltpu.roll(out_part, CODE, 1),
        in_part + pltpu.roll(in_part, CODE, 1),
    )


def project(seeds, queries, hidden, grads):
    hbm = pl.BlockSpec(memory_space=pltpu.HBM)
    depth = (hidden.shape[1] + grads.shape[1]) // 2
    return pl.pallas_call(
        project_kernel,
        in_specs=[SMEM, VMEM, hbm, hbm],
        out_specs=[VMEM, VMEM],
        out_shape=[
            jax.ShapeDtypeStruct((hidden.shape[0], 2 * CODE), F32),
            jax.ShapeDtypeStruct((32, CODE // 2, 2 * CODE), queries.dtype),
        ],
        scratch_shapes=[
            pltpu.VMEM(hidden.shape, hidden.dtype),
            pltpu.VMEM(grads.shape, grads.dtype),
            pltpu.VMEM((depth, 2 * CODE), jnp.bfloat16),
            pltpu.SemaphoreType.DMA((2 * STEPS + 1,)),
        ],
        compiler_params=pltpu.CompilerParams(vmem_limit_bytes=127 * 2**19),
        name="project",
    )(seeds, queries, hidden, grads)


def codes_kernel(lengths_ref, own_ref, other_ref, made_ref):
    total = own_ref[...] + other_ref[...]
    tokens = total.shape[0] // 2
    position = lax.broadcasted_iota(I32, (tokens, 1), 0)
    codes = []
    for e in range(2):
        length = lengths_ref[e]
        scale = (1.0 / math.sqrt(D)) * (1.0 / math.sqrt(FF))
        weight = jnp.where(position < length, scale / length.astype(F32), 0.0)
        part = total[e * tokens : (e + 1) * tokens]
        both = dot(part * weight, part, ((0,), (0,)))
        codes.append(both[:CODE, CODE:])
    wide = jnp.concatenate(codes, axis=1)
    tall = jnp.concatenate(codes, axis=0)
    made_ref[PACKED[0] : PACKED[0] + CODE] = wide
    out_factor = dot(wide, wide, ((1,), (1,)))
    in_factor = dot(tall, tall, ((0,), (0,)))
    row = lax.broadcasted_iota(I32, (CODE, CODE), 0)
    col = lax.broadcasted_iota(I32, (CODE, CODE), 1)
    square = jnp.where(col >= row, out_factor, in_factor)
    half = CODE // 2
    made_ref[:half] = jnp.concatenate([square[:half], square[half:]], axis=1)
    diagonal = jnp.sum(jnp.where(row == col, in_factor, 0.0), axis=0, keepdims=True)
    tail = jnp.concatenate([diagonal, jnp.zeros_like(diagonal)], axis=1)
    made_ref[half : PACKED[0]] = jnp.broadcast_to(tail, (8, 2 * CODE))


def hold_kernel(own_ref, held_ref):
    held_ref[...] = own_ref[...]


def hold(own):
    return pl.pallas_call(
        hold_kernel,
        in_specs=[VMEM],
        out_specs=VMEM,
        out_shape=jax.ShapeDtypeStruct(own.shape, own.dtype),
        compiler_params=SMALL,
        cost_estimate=pl.CostEstimate(flops=HOLD_FLOPS, bytes_accessed=0, transcendentals=0),
        name="hold",
    )(own)


def make_codes(lengths, own, other):
    return pl.pallas_call(
        codes_kernel,
        in_specs=[SMEM, VMEM, VMEM],
        out_specs=VMEM,
        out_shape=jax.ShapeDtypeStruct((PACKED[0] + CODE, 2 * CODE), F32),
        compiler_params=SMALL,
        cost_estimate=pl.CostEstimate(flops=CODES_FLOPS, bytes_accessed=0, transcendentals=0),
        name="codes",
    )(lengths, own, other)


def add_kernel(*refs):
    copies_ref = refs[-1]
    if len(refs) == 3:
        packed = slice(0, PACKED[0])
        total = refs[0][packed] + refs[1][packed]
    else:
        total = refs[0][0]
        for i in range(1, refs[0].shape[0]):
            total = total + refs[0][i]
    for i in range(copies_ref.shape[0]):
        copies_ref[i] = total


def add_and_copy(count, *arrays):
    return pl.pallas_call(
        add_kernel,
        in_specs=[VMEM] * len(arrays),
        out_specs=VMEM,
        out_shape=jax.ShapeDtypeStruct((count,) + PACKED, F32),
        compiler_params=SMALL,
        name="add",
    )(*arrays)


def invert_both(grid):
    rows = 8
    lane = lax.broadcasted_iota(I32, (rows, 2 * CODE), 1)
    sub = lax.broadcasted_iota(I32, (rows, 2 * CODE), 0)
    place = lane & (CODE - 1)
    first = lane - place

    def columns_of(parts, k):
        return [
            [jnp.take_along_axis(part, first + (k + i), axis=1) for part in parts]
            for i in range(2)
        ]

    parts = [grid[i : i + rows] for i in range(0, CODE, rows)]
    left, right = columns_of(parts, 0)
    for k in range(0, CODE, 2):
        at, s = divmod(k, rows)
        a, b = left[at][s : s + 1], right[at][s : s + 1]
        c, d = left[at][s + 1 : s + 2], right[at][s + 1 : s + 2]
        scale = 1.0 / (a * d - b * c)
        a, b, c, d = d * scale, -b * scale, -c * scale, a * scale

        def pivot_rows(parts):
            one, two = parts[at][s : s + 1], parts[at][s + 1 : s + 2]
            return a * one + b * two, c * one + d * two

        def update(parts, one, two):
            parts = [p - l * one - r * two for p, l, r in zip(parts, left, right)]
            parts[at] = jnp.where(sub == s, one, jnp.where(sub == s + 1, two, parts[at]))
            return parts

        if k + 2 < CODE:
            later = [update(new, *pivot_rows(new)) for new in columns_of(parts, k + 2)]
        one, two = pivot_rows(parts)
        one = jnp.where(place[:1] == k, a, jnp.where(place[:1] == k + 1, b, one))
        two = jnp.where(place[:1] == k, c, jnp.where(place[:1] == k + 1, d, two))
        here = (place == k) | (place == k + 1)
        parts = update([jnp.where(here, 0.0, part) for part in parts], one, two)
        left, right = later
    return jnp.concatenate(parts, axis=0)


def condition_kernel(parts_ref, own_ref, other_ref, here_ref, there_ref, rows_ref, lines_ref):
    packed = parts_ref[0]
    for i in range(1, parts_ref.shape[0]):
        packed = packed + parts_ref[i]
    half = CODE // 2
    square = jnp.concatenate([packed[:half, :CODE], packed[:half, CODE:]], axis=0)
    row = lax.broadcasted_iota(I32, (CODE, CODE), 0)
    col = lax.broadcasted_iota(I32, (CODE, CODE), 1)
    upper = jnp.where(col > row, square, 0.0)
    lower = jnp.where(col < row, square, 0.0)
    diagonal = jnp.where(col == row, square, 0.0)
    trace = jnp.sum(diagonal)
    out_factor = upper + upper.T + diagonal
    in_factor = lower + lower.T + jnp.where(col == row, packed[half : half + 1, :CODE], 0.0)

    row = lax.broadcasted_iota(I32, (CODE, 2 * CODE), 0)
    lane = lax.broadcasted_iota(I32, (CODE, 2 * CODE), 1)
    grid = jnp.concatenate([out_factor, in_factor], axis=1) * (CODE / trace)
    grid = grid + jnp.where((lane & (CODE - 1)) == row, DAMPING, 0.0)
    grid = invert_both(grid)
    out_inverse = grid[:, :CODE]
    in_inverse = grid[:, CODE:]
    nn = ((1,), (0,))
    score_scale = 1.0 / math.sqrt(CODE)
    scaled = in_inverse * score_scale
    core = lax.axis_index("cuts")
    mine = pl.ds(pl.multiple_of(core * (half // 2), 8), half // 2)
    for ref, flat_ref in ((own_ref, here_ref), (other_ref, there_ref)):
        left = dot(out_inverse, ref[PACKED[0] : PACKED[0] + CODE], nn)
        rows_ref[:, :CODE] = dot(left[:, :CODE], scaled, nn)
        rows_ref[:, CODE:] = dot(left[:, CODE:], scaled, nn)
        even = rows_ref[pl.ds(0, half, stride=2), :]
        odd = rows_ref[pl.ds(1, half, stride=2), :]
        lines_ref[:, :CODE] = even[:, :CODE]
        lines_ref[:, CODE:] = odd[:, :CODE]
        flat_ref[0] = lines_ref[mine]
        lines_ref[:, :CODE] = even[:, CODE:]
        lines_ref[:, CODE:] = odd[:, CODE:]
        flat_ref[1] = lines_ref[mine]


def condition(parts, own, other):
    half = CODE // 2
    return pl.pallas_call(
        condition_kernel,
        in_specs=[VMEM] * 3,
        out_specs=[VMEM, VMEM],
        out_shape=[jax.ShapeDtypeStruct((2, half // 2, 2 * CODE), F32)] * 2,
        scratch_shapes=[
            pltpu.VMEM((CODE, 2 * CODE), F32),
            pltpu.VMEM((half, 2 * CODE), F32),
        ],
        compiler_params=SMALL,
        cost_estimate=pl.CostEstimate(flops=CONDITION_FLOPS, bytes_accessed=0, transcendentals=0),
        name="condition",
    )(parts, own, other)


def row_sums(arrays):
    sub = lax.broadcasted_iota(I32, (8, 2 * CODE), 0)
    for shift in (1, 2, 4):
        low = (sub & shift) == 0
        arrays = [
            jnp.where(low, a, b) + pltpu.roll(jnp.where(low, b, a), shift, 0)
            for a, b in zip(arrays[::2], arrays[1::2])
        ]
    return arrays[0]


def score_kernel(flat_ref, *refs):
    *queries_refs, out_ref, sums = refs
    width = 2 * CODE
    depth = flat_ref.shape[1]
    flat = [flat_ref[e] for e in range(2)]
    x = lax.axis_index("x")
    places = len(queries_refs)
    for behind, queries_ref in enumerate(queries_refs):
        count = 2 * queries_ref.shape[0]
        came = lax.rem(x + (places - behind), places) * count
        for group in range(0, count, 8):
            products = [[], []]
            for q in range(group, group + 8):
                first = (q % 2) * depth
                query = queries_ref[q // 2, first : first + depth].astype(F32)
                for e in range(2):
                    product = query * flat[e]
                    products[e].append(product[: depth // 2] + product[depth // 2 :])
            place = pl.ds(pl.multiple_of(came + group, 8), 8)
            for e in range(2):
                sums[e, place] = row_sums(products[e])
    ones = jnp.ones((8, width), F32)
    for e in range(2):
        out_ref[e : e + 1] = dot(ones, sums[e], ((1,), (1,)))[:1]


def score(flat, queries):
    count = sum(2 * q.shape[0] for q in queries)
    return pl.pallas_call(
        score_kernel,
        in_specs=[VMEM] * (1 + len(queries)),
        out_specs=VMEM,
        out_shape=jax.ShapeDtypeStruct((2, count), F32),
        scratch_shapes=[pltpu.VMEM((2, count, 2 * CODE), F32)],
        compiler_params=SMALL,
        cost_estimate=pl.CostEstimate(flops=10**9, bytes_accessed=0, transcendentals=0),
        name="score",
    )(flat, *queries)


def join_kernel(here_ref, there_ref, out_ref):
    out_ref[...] = here_ref[...] + there_ref[...]


def join(here, there):
    return pl.pallas_call(
        join_kernel,
        in_specs=[VMEM, VMEM],
        out_specs=VMEM,
        out_shape=jax.ShapeDtypeStruct(here.shape, F32),
        compiler_params=SMALL,
        name="join",
    )(here, there)


SWAP = [(0, 1), (1, 0)]


def on_device(hidden, out_grads, lengths, queries, proj_seeds):
    examples, seq_len, ff_local = hidden.shape
    d_local = out_grads.shape[2]
    own, copies = project(
        proj_seeds, queries, hidden.reshape(-1, ff_local), out_grads.reshape(-1, d_local)
    )
    other = lax.ppermute(own, "mp", SWAP)
    near = lax.all_to_all(copies, ("y", "z"), 0, 0)
    made = make_codes(lengths, hold(own), other)
    made_there = lax.ppermute(made, "cuts", SWAP)
    total = add_and_copy(16, made, made_there)
    total, near = lax.optimization_barrier((total, near))
    up = [(i, (i + 1) % 4) for i in range(4)]
    down = [(i, (i + 3) % 4) for i in range(4)]
    from_below = lax.ppermute(near, "x", up)
    from_above = lax.ppermute(near, "x", down)
    from_below, from_above = lax.optimization_barrier((from_below, from_above))
    from_across = lax.ppermute(from_below, "x", up)
    all_queries = [near, from_below, from_across, from_above]
    copies = add_and_copy(8, lax.all_to_all(total, ("x", "y"), 0, 0))
    parts = lax.all_to_all(copies, "z", 0, 0)
    flat_here, flat_there = condition(parts, made, made_there)
    arrived = lax.ppermute(score(flat_there, all_queries), "cuts", SWAP)
    return join(score(flat_here, all_queries), arrived)


def solution(mesh):
    fine = Mesh(mesh.devices.reshape(2, 4, 4, 8, 2), ("cuts", "x", "y", "z", "mp"))
    rows = ("cuts", "x", "y", "z")
    return jax.shard_map(
        on_device,
        mesh=fine,
        in_specs=(
            P(rows, None, "mp"),
            P(rows, None, "mp"),
            P(rows),
            P(("x", "y", "z"), None),
            P(),
        ),
        out_specs=P(rows, None),
        check_vma=False,
    )
```
